32 devices in a mesh: tx: 8 (over z, core), gx: 2 (over x), gy: 2 (over y).
Axes of the slice: x: 2, y: 2, z: 4, core: 2. Of those that a mesh axis runs over, the one named last changes fastest.
Arguments:
- cond_h: float32 [32, 32, 128], P('gx', 'gy'), may hold values from 0.1 to 1.5
- cond_v: float32 [32, 32, 128], P('gx', 'gy'), may hold values from 0.1 to 1.5
- fwd_init: float32 [8, 6, 32, 32, 128], P('tx', None, 'gx', 'gy'), may hold values from -6 to 6
- adj_init: float32 [8, 6, 32, 32, 128], P('tx', None, 'gx', 'gy'), may hold values from -6 to 6
- observed: float32 [8, 4, 2, 2, 2, 32], P('tx', None, 'gx', 'gy'), may hold values from -6 to 6
- footprint: int32 [8, 2, 2], P('tx', 'gx', 'gy'), may hold values 0 or 1
- owner: int32 [2, 2, 8], P('gx', 'gy'), may hold values from 0 to 7, each once within a row
- rec_cells: int32 [2, 2, 32], P('gx', 'gy'), may hold values from 0 to 255
Outputs:
- owned_gradient: float32 [2, 8, 2, 2, 32, 128], P('gx', 'tx', None, None, 'gy')
- misfit: float32 [], replicated
The draws below stay inside these ranges and needn't reach their ends.
Inputs may be any that keep to these rules, and one draw needn't show every extreme that they name: `owner`: each tile's row is a permutation of 0 to 7. `rec_cells`: cell index x * 16 + y within the tile; receivers may share a cell. `footprint`: 1 where the group's gradient counts in the tile.
All inputs are finite; a program needn't handle non-finite values.
Results may differ from the reference program's by a relative error of at most 0.00028.
Values sent between devices are 32-bit elements; how exact they have to be, the bound alone decides.
A program may use at most 64 MiB of HBM per device.

```python
import math
import jax
import jax.numpy as jnp
from jax import lax

CX = 16
CY = 16
NZ = 128
RPT = 32
STEPS = 4
ZREC = 32
GROUPS = 8
TILES_X = 2
TILES_Y = 2
NX = 32
NY = 32
XB = 2
N_TX = 8


def set_ends(values, stream_key, smallest, top_value):
    place = [jax.random.randint(jax.random.fold_in(stream_key, axis), (), 0, length) for axis, length in enumerate(values.shape)]
    widest = values.shape.index(max(values.shape))
    beside = place[:widest] + [(place[widest] + 1) % values.shape[widest]] + place[widest + 1:]
    return values.at[tuple(place)].set(smallest).at[tuple(beside)].set(top_value)


def block_levels(stream_key, shape, split, smallest, top_value):
    factor_of, own = 1.0, jax.random.fold_in(stream_key, 6)
    for dim, shards_of in split:
        steps = jnp.exp(jax.random.uniform(jax.random.fold_in(own, dim), (shards_of,), jnp.float32, smallest / len(split), top_value / len(split)))
        factor_of = factor_of * jnp.repeat(steps, shape[dim] // shards_of).reshape([-1 if axis == dim else 1 for axis in range(len(shape))])
    return factor_of


def normal_values(key, shape, width, bound, split=(), kind=jnp.bfloat16):
    factor_of = block_levels(key, shape, split, -0.22, 0.18) if split else 1.0
    drawn = jax.random.normal(key, shape, jnp.float32) * width * factor_of
    return jnp.minimum(jnp.maximum(drawn, -bound), bound).astype(kind)


def setup_inputs(seed: int = 0) -> dict:
    arg_keys = jax.random.split(jax.random.key(seed), 9)
    cond_h = jnp.clip(jnp.exp(math.log(1.5) - 2.7080502 * jax.random.uniform(arg_keys[0], (NX, NY, NZ), jnp.float32) ** block_levels(arg_keys[0], (NX, NY, NZ), ((0, 2), (1, 2)), -0.2, 0.2)), 0.1, 1.5)
    cond_v = jnp.clip(jnp.exp(math.log(1.5) - 2.7080502 * jax.random.uniform(arg_keys[1], (NX, NY, NZ), jnp.float32) ** block_levels(arg_keys[1], (NX, NY, NZ), ((0, 2), (1, 2)), -0.2, 0.2)), 0.1, 1.5)
    fwd_init = normal_values(arg_keys[2], (GROUPS, 6, NX, NY, NZ), 1.0, 6.0, ((0, 8), (2, 2), (3, 2)), jnp.float32)
    adj_init = normal_values(arg_keys[3], (GROUPS, 6, NX, NY, NZ), 1.0, 6.0, ((0, 8), (2, 2), (3, 2)), jnp.float32)
    observed = normal_values(arg_keys[4], (GROUPS, STEPS, TILES_X, TILES_Y, 2, RPT), 1.0, 6.0, ((0, 8), (2, 2), (3, 2)), jnp.float32)
    footprint = set_ends((jax.random.randint(arg_keys[5], (GROUPS, TILES_X, TILES_Y), 0, 4) < 3).astype(jnp.int32), jax.random.fold_in(arg_keys[5], 1), 0, 1)
    owner = jax.vmap(lambda own: jax.random.permutation(own, GROUPS))(jax.random.split(arg_keys[6], TILES_X * TILES_Y)).reshape((TILES_X, TILES_Y, GROUPS)).astype(jnp.int32)
    rec_cells = set_ends(jax.random.randint(arg_keys[7], (TILES_X, TILES_Y, RPT), 0, CX * CY), jax.random.fold_in(arg_keys[7], 1), 0, (CX * CY) - 1).astype(jnp.int32)
    return {"cond_h": cond_h, "cond_v": cond_v, "fwd_init": fwd_init, "adj_init": adj_init, "observed": observed, "footprint": footprint, "owner": owner, "rec_cells": rec_cells}


STEP_DT = 0.5


def coefficients(conduct):
    half_rate = 0.25 * conduct
    return (1.0 - half_rate) / (1.0 + half_rate), STEP_DT / (1.0 + half_rate)


def ahead_of(values, axis_num):
    extent = values.shape[axis_num]
    tail_plane = jnp.zeros_like(lax.slice_in_dim(values, 0, 1, axis=axis_num))
    return jnp.concatenate([lax.slice_in_dim(values, 1, extent, axis=axis_num), tail_plane], axis=axis_num)


def before(values, axis_num):
    extent = values.shape[axis_num]
    head_plane = jnp.zeros_like(lax.slice_in_dim(values, 0, 1, axis=axis_num))
    return jnp.concatenate([head_plane, lax.slice_in_dim(values, 0, extent - 1, axis=axis_num)], axis=axis_num)


def curl_ahead(field):
    comp_x, comp_y, comp_z = field[0], field[1], field[2]
    out_x = (ahead_of(comp_z, 1) - comp_z) - (ahead_of(comp_y, 2) - comp_y)
    out_y = (ahead_of(comp_x, 2) - comp_x) - (ahead_of(comp_z, 0) - comp_z)
    out_z = (ahead_of(comp_y, 0) - comp_y) - (ahead_of(comp_x, 1) - comp_x)
    return jnp.stack([out_x, out_y, out_z])


def curl_before(field):
    comp_x, comp_y, comp_z = field[0], field[1], field[2]
    out_x = (comp_z - before(comp_z, 1)) - (comp_y - before(comp_y, 2))
    out_y = (comp_x - before(comp_x, 2)) - (comp_z - before(comp_z, 0))
    out_z = (comp_y - before(comp_y, 0)) - (comp_x - before(comp_x, 1))
    return jnp.stack([out_x, out_y, out_z])


def reference(cond_h, cond_v, fwd_init, adj_init, observed, footprint, owner, rec_cells):
    decay_h, drive_h = coefficients(cond_h)
    decay_v, drive_v = coefficients(cond_v)
    decay = jnp.stack([decay_h, decay_h, decay_v])
    drive = jnp.stack([drive_h, drive_h, drive_v])
    cell_ids = jnp.arange(CX * CY, dtype=jnp.int32)
    onehot = (rec_cells[..., None] == cell_ids).astype(jnp.float32)
    highest = lax.Precision.HIGHEST

    def record(electric):
        planes = electric[0:2, :, :, ZREC].reshape(2, TILES_X, CX, TILES_Y, CY)
        planes = planes.transpose(0, 1, 3, 2, 4).reshape(2, TILES_X, TILES_Y, CX * CY)
        return jnp.einsum("cabk,abrk->abcr", planes, onehot, precision=highest)

    def inject(electric, residual):
        spread = jnp.einsum("abcr,abrk->cabk", residual, onehot, precision=highest)
        spread = spread.reshape(2, TILES_X, TILES_Y, CX, CY).transpose(0, 1, 3, 2, 4).reshape(2, NX, NY)
        return electric.at[0:2, :, :, ZREC].add(spread)

    def one_group(state_pair, inputs):
        summed_grad, misfit_sum = state_pair
        forward, adjoint, observe, tile_flags = inputs
        electric, magnetic = forward[0:3], forward[3:6]
        stored = []
        residuals = []
        for step_idx in range(STEPS):
            magnetic = magnetic - STEP_DT * curl_ahead(electric)
            electric = decay * electric + drive * curl_before(magnetic)
            stored.append(electric)
            residuals.append(record(electric) - observe[step_idx])
        local_misfit = jnp.float32(0.0)
        for step_idx in range(STEPS):
            local_misfit = local_misfit + 0.5 * jnp.sum(residuals[step_idx] * residuals[step_idx])
        adj_e, adj_h = adjoint[0:3], adjoint[3:6]
        grad_h = jnp.zeros((NX, NY, NZ), jnp.float32)
        grad_v = jnp.zeros((NX, NY, NZ), jnp.float32)
        for step_idx in reversed(range(STEPS)):
            adj_e = inject(adj_e, residuals[step_idx])
            adj_h = adj_h - STEP_DT * curl_ahead(adj_e)
            adj_e = decay * adj_e + drive * curl_before(adj_h)
            kept = stored[step_idx]
            grad_h = grad_h + adj_e[0] * kept[0] + adj_e[1] * kept[1]
            grad_v = grad_v + adj_e[2] * kept[2]
        tile_mask = jnp.repeat(jnp.repeat(tile_flags.astype(jnp.float32), CX, axis=0), CY, axis=1)[:, :, None]
        summed_grad = summed_grad + jnp.stack([grad_h, grad_v]) * tile_mask
        return (summed_grad, misfit_sum + local_misfit), None

    start = (jnp.zeros((2, NX, NY, NZ), jnp.float32), jnp.float32(0.0))
    (summed_grad, misfit), _ = lax.scan(one_group, start, (fwd_init, adj_init, observed, footprint))
    blocked = summed_grad.reshape(2, TILES_X, N_TX, XB, TILES_Y, CY, NZ).transpose(1, 4, 2, 0, 3, 5, 6)
    chosen = jnp.take_along_axis(blocked, owner[:, :, :, None, None, None, None].astype(jnp.int32), axis=2)
    owned_part = chosen.transpose(0, 2, 3, 4, 1, 5, 6).reshape(TILES_X, N_TX, 2, XB, NY, NZ)
    return owned_part, misfit
```

```python
import functools

import jax
import jax.numpy as jnp
from jax import lax
from jax.experimental import pallas as pl
from jax.experimental.pallas import tpu as pltpu
from jax.sharding import PartitionSpec as P

STEPS = 4
ZREC = 32
STEP_DT = 0.5
HALO = STEPS
LOW = HALO + 1
CHUNK = 4
MESH = pl.DeviceIdType.MESH
DIRS = [(dx, dy) for dx in (-1, 0, 1) for dy in (-1, 0, 1) if (dx, dy) != (0, 0)]


def window_rows(gx_size, size_x):
    return size_x + (HALO if gx_size == 2 else 2 * HALO)


def kernel(
    sizes,
    cond_h, cond_v, fwd, adj, observed, footprint, owner, rec_cells,
    out, misfit_out,
    fw, aw, cw, decay, drive, kept, grad, inj_own, inj_in, inj_win, obs_scr,
    mis_own, mis_in, give, keep, got, part,
    loc_sem, halo_send, halo_recv, inj_send, inj_recv, mis_send, mis_recv,
    sib_send, sib_recv, z_send, z_recv,
):
    n_tx, n_gx, n_gy = sizes
    nz = n_tx // 2
    size_x, size_y, depth = cond_h.shape
    rows_w = window_rows(n_gx, size_x)
    wy = size_y + 2 * HALO
    it, ix, iy = lax.axis_index("tx"), lax.axis_index("gx"), lax.axis_index("gy")
    core = lax.rem(it, 2)
    iz = it // 2
    has = {}
    for dx, dy in DIRS:
        ok = None
        for d, i, n in ((dx, ix, n_gx), (dy, iy, n_gy)):
            if d:
                one = (i > 0) if d < 0 else (i < n - 1)
                ok = one if ok is None else jnp.logical_and(ok, one)
        has[(dx, dy)] = ok
    has_lo, has_hi = has[(-1, 0)], has[(1, 0)]
    start = jnp.where(has_lo, -HALO, 0)

    def plane_partner(k):
        ox, oy = k // n_gy, k % n_gy
        return {"gx": lax.rem(ix + ox, n_gx), "gy": lax.rem(iy + oy, n_gy)}

    sibling = {"tx": it + 1 - 2 * core}

    def z_partner(dz):
        return lax.rem(iz + dz, nz)

    tile_x, tile_y = pl.ds(LOW, size_x), pl.ds(0, size_y)
    locals_ = [
        pltpu.make_async_copy(cond_h, cw.at[0, tile_x, tile_y], loc_sem.at[0]),
        pltpu.make_async_copy(cond_v, cw.at[1, tile_x, tile_y], loc_sem.at[1]),
        pltpu.make_async_copy(fwd.at[0], fw.at[:, tile_x, tile_y], loc_sem.at[2]),
        pltpu.make_async_copy(adj.at[0], aw.at[:, tile_x, tile_y], loc_sem.at[3]),
    ]
    for c in locals_:
        c.start()

    rows_all = fw.shape[1]
    for ref in (cw, fw, aw):
        comps = ref.shape[0]
        ref[:, 0:LOW] = jnp.zeros((comps, LOW, wy, depth), jnp.float32)
        top = LOW + size_x
        ref[:, top:rows_all] = jnp.zeros((comps, rows_all - top, wy, depth), jnp.float32)
        ref[:, LOW:top, size_y:wy] = jnp.zeros((comps, size_x, wy - size_y, depth), jnp.float32)
    inj_in[...] = jnp.zeros_like(inj_in)

    barrier = pltpu.get_barrier_semaphore()
    for k in range(1, n_gx * n_gy):
        pl.semaphore_signal(barrier, inc=1, device_id=plane_partner(k), device_id_type=MESH)
    pl.semaphore_signal(barrier, inc=1, device_id=sibling, device_id_type=MESH)
    for dz in range(1, nz):
        pl.semaphore_signal(
            barrier, inc=1, device_id={"tx": 2 * z_partner(dz) + core}, device_id_type=MESH
        )
    pl.semaphore_wait(barrier, n_gx * n_gy - 1 + 1 + nz - 1)

    def source(d, size):
        return pl.ds(0, size) if d == 0 else (pl.ds(size - HALO, HALO) if d > 0 else pl.ds(0, HALO))

    def target_x(d):
        return tile_x if d == 0 else (pl.ds(LOW - HALO, HALO) if d > 0 else pl.ds(LOW + size_x, HALO))

    def target_y(d):
        return tile_y if d == 0 else (pl.ds(size_y + HALO, HALO) if d > 0 else pl.ds(size_y, HALO))

    def halo_copy(which, d):
        dx, dy = DIRS[d]
        sx, sy = source(dx, size_x), source(dy, size_y)
        tx_, ty_ = target_x(dx), target_y(dy)
        src, dst = {
            0: (cond_h.at[sx, sy], cw.at[0, tx_, ty_]),
            1: (cond_v.at[sx, sy], cw.at[1, tx_, ty_]),
            2: (fwd.at[0, :, sx, sy], fw.at[:, tx_, ty_]),
            3: (adj.at[0, :, sx, sy], aw.at[:, tx_, ty_]),
        }[which]
        return pltpu.make_async_remote_copy(
            src_ref=src, dst_ref=dst,
            send_sem=halo_send.at[which, d], recv_sem=halo_recv.at[which, d],
            device_id={"gx": ix + dx, "gy": iy + dy}, device_id_type=MESH,
        )

    def each_dir(fn, conds):
        for d, (dx, dy) in enumerate(DIRS):
            if (dx and n_gx == 1) or (dy and n_gy == 1):
                continue
            pl.when(conds(dx, dy))(functools.partial(fn, d))

    def to_side(dx, dy):
        return has[(dx, dy)]

    def from_side(dx, dy):
        return has[(-dx, -dy)]

    for which in range(4):
        each_dir(lambda d, w=which: halo_copy(w, d).start(), to_side)

    lanes = lax.broadcasted_iota(jnp.int32, (size_y, depth), 1)
    highest = lax.Precision.HIGHEST
    rpt = rec_cells.shape[-1]
    cells = rec_cells[0]
    in_y = (lax.broadcasted_iota(jnp.int32, (size_y, rpt), 0) == cells % size_y).astype(jnp.float32)
    in_x = (lax.broadcasted_iota(jnp.int32, (size_x, rpt), 0) == cells // size_y).astype(jnp.float32)
    lane_x = (
        lax.broadcasted_iota(jnp.int32, (size_x, depth), 0)
        == lax.broadcasted_iota(jnp.int32, (size_x, depth), 1) % size_x
    ).astype(jnp.float32)
    lane_k = (
        lax.broadcasted_iota(jnp.int32, (2 * STEPS, depth), 0)
        == lax.broadcasted_iota(jnp.int32, (2 * STEPS, depth), 1) // size_x
    ).astype(jnp.float32)
    for n in range(STEPS):
        obs_scr[2 * n : 2 * n + 2, 0:rpt] = observed[0, n, 0, 0]
    over0 = (((0,), (0,)), ((), ()))
    at_x = lax.dot_general(in_x, lane_x, over0, precision=highest, preferred_element_type=jnp.float32)
    obs_l = at_x * lax.dot_general(
        obs_scr[:, 0:rpt], lane_k, over0, precision=highest, preferred_element_type=jnp.float32
    )
    count = jnp.dot(in_y, at_x, precision=highest, preferred_element_type=jnp.float32)
    obs_sum = jnp.dot(in_y, obs_l, precision=highest, preferred_element_type=jnp.float32)

    for n in range(STEPS):
        for x in sorted({size_x, size_x + HALO, rows_w}):
            kept[n, :, LOW + x] = jnp.zeros((3, wy, depth), jnp.float32)

    def wait_in(which):
        locals_[which].wait()
        each_dir(lambda d: halo_copy(which, d).wait_recv(), from_side)

    wait_in(0)
    wait_in(1)
    sub = lax.broadcasted_iota(jnp.int32, (wy, depth), 0)
    lane = lax.broadcasted_iota(jnp.int32, (wy, depth), 1)
    y_hi = jnp.where(has[(0, 1)], 1.0, 0.0)
    y_lo = jnp.where(has[(0, -1)], 1.0, 0.0)
    y_ok = jnp.where(sub < size_y, 1.0, jnp.where(sub < size_y + HALO, y_hi, y_lo))
    half = STEP_DT * y_ok
    chunks = rows_w // CHUNK

    def coefficients(k, carry):
        for i in range(CHUNK):
            x = start + k * CHUNK + i
            ok = y_ok * jnp.where(jnp.logical_or(x < size_x, has_hi), 1.0, 0.0)
            for c in range(2):
                rate = 0.25 * cw[c, x + LOW]
                scaled = ok / (1.0 + rate)
                drive[c, x + LOW] = STEP_DT * scaled
                decay[c, x + LOW] = (1.0 - rate) * scaled
        return carry

    lax.fori_loop(0, chunks, coefficients, 0)

    def y_next(f):
        return pltpu.roll(f, wy - 1, 0)

    def y_prev(f):
        return pltpu.roll(f, 1, 0)

    def z_next(f):
        return jnp.where(lane == depth - 1, 0.0, pltpu.roll(f, depth - 1, 1))

    def z_prev(f):
        return jnp.where(lane == 0, 0.0, pltpu.roll(f, 1, 1))

    def step_rows(r, e_src, h, e_dst, after):
        e = [[e_src[c, r + i] for c in range(3)] for i in range(CHUNK)]
        last = r + CHUNK
        e.append([None, e_src[1, last], e_src[2, last]])
        hp_y, hp_z = h[1, r - 1], h[2, r - 1]
        for i in range(CHUNK):
            ex, ey, ez = e[i]
            _, ey_n, ez_n = e[i + 1]
            hx = h[0, r + i] - half * ((y_next(ez) - ez) - (z_next(ey) - ey))
            hy = h[1, r + i] - half * ((z_next(ex) - ex) - (ez_n - ez))
            hz = h[2, r + i] - half * ((ey_n - ey) - (y_next(ex) - ex))
            h[0, r + i] = hx
            h[1, r + i] = hy
            h[2, r + i] = hz
            cx = (hz - y_prev(hz)) - (hy - z_prev(hy))
            cy = (hx - z_prev(hx)) - (hz - hp_z)
            cz = (hy - hp_y) - (hx - y_prev(hx))
            hp_y, hp_z = hy, hz
            dec_h, drv_h = decay[0, r + i], drive[0, r + i]
            dec_v, drv_v = decay[1, r + i], drive[1, r + i]
            new = (dec_h * ex + drv_h * cx, dec_h * ey + drv_h * cy, dec_v * ez + drv_v * cz)
            for c in range(3):
                e_dst[c, r + i] = new[c]
            if after is not None:
                after(r + i, new)

    def step(e_src, h, e_dst, after=None):
        def body(k, carry):
            step_rows(start + LOW + k * CHUNK, e_src, h, e_dst, after)
            return carry

        lax.fori_loop(0, chunks, body, 0)

    wait_in(2)
    for n in range(STEPS):
        step(fw.at[0:3] if n == 0 else kept.at[n - 1], fw.at[3:6], kept.at[n])

    rec = jnp.zeros((size_y, depth), jnp.float32)
    for n in range(STEPS):
        for c in range(2):
            for x in range(size_x):
                at = (2 * n + c) * size_x + x
                e = kept[n, c, LOW + x, 0:size_y]
                rec = jnp.where(lanes == at, pltpu.roll(e, (at - ZREC) % depth, 1), rec)
    inj_own[...] = count * rec - obs_sum

    def inj_copy(d):
        dx, dy = DIRS[d]
        return pltpu.make_async_remote_copy(
            src_ref=inj_own, dst_ref=inj_in.at[(1 - dx) * 3 + 1 - dy],
            send_sem=inj_send.at[d], recv_sem=inj_recv.at[d],
            device_id={"gx": ix + dx, "gy": iy + dy}, device_id_type=MESH,
        )

    each_dir(lambda d: inj_copy(d).start(), to_side)

    at_rec = lax.dot_general(in_y, rec, over0, precision=highest, preferred_element_type=jnp.float32)
    resid = at_x * at_rec - obs_l
    mis_own[...] = 0.5 * jnp.sum((resid * resid).reshape(rpt // 8, 8, depth), axis=0)

    def mis_copy(k):
        return pltpu.make_async_remote_copy(
            src_ref=mis_own, dst_ref=mis_in.at[k],
            send_sem=mis_send.at[k], recv_sem=mis_recv.at[k],
            device_id=plane_partner(k), device_id_type=MESH,
        )

    for k in range(1, n_gx * n_gy):
        mis_copy(k).start()

    wait_in(3)
    each_dir(lambda d: inj_copy(d).wait_recv(), from_side)
    sub8 = lax.broadcasted_iota(jnp.int32, (2 * HALO, depth), 0)
    for q in range(3):
        own = inj_own[...] if q == 1 else inj_in[q * 3 + 1]
        inj_win[q, 0:size_y] = own
        inj_win[q, size_y:wy] = jnp.where(
            sub8 < HALO,
            inj_in[q * 3 + 2, 0 : 2 * HALO],
            inj_in[q * 3, size_y - 2 * HALO : size_y],
        )

    for n in reversed(range(STEPS)):

        def inject(k, carry, n=n):
            for i in range(CHUNK):
                x = start + k * CHUNK + i
                plane = inj_win[(x + size_x) // size_x]
                for c in range(2):
                    at = (2 * n + c) * size_x + lax.rem(x + size_x, size_x)
                    moved = pltpu.roll(plane, lax.rem(ZREC + depth - at, depth), 1)
                    aw[c, x + LOW] = aw[c, x + LOW] + jnp.where(lane == ZREC, moved, 0.0)
            return carry

        lax.fori_loop(0, chunks, inject, 0)

        def add_gradient(r, new, n=n):
            tile = slice(0, size_y)
            g_h = new[0][tile] * kept[n, 0, r, tile] + new[1][tile] * kept[n, 1, r, tile]
            g_v = new[2][tile] * kept[n, 2, r, tile]
            if n < STEPS - 1:
                g_h = grad[0, r] + g_h
                g_v = grad[1, r] + g_v
            grad[0, r] = g_h
            grad[1, r] = g_v

        step(aw.at[0:3], aw.at[3:6], aw.at[0:3], add_gradient)

    for k in range(1, n_gx * n_gy):
        mis_copy(k).wait_recv()
    misfit = mis_own[...]
    for k in range(1, n_gx * n_gy):
        misfit = misfit + mis_in[k]

    flag = footprint[0, 0, 0].astype(jnp.float32)
    block = size_x // n_tx
    cells_rows = 2 * block * size_y

    def ordered(dst, dz, to_core):
        z = z_partner(dz)
        first = owner[0, 0, 2 * z + to_core] * block
        for c in range(2):
            for b in range(block):
                at = (c * block + b) * size_y
                dst[dz, at : at + size_y] = flag * grad[c, LOW + first + b]
        dst[dz, cells_rows : cells_rows + 8] = misfit

    def sib_copy(dz):
        return pltpu.make_async_remote_copy(
            src_ref=give.at[dz], dst_ref=got.at[dz],
            send_sem=sib_send.at[dz], recv_sem=sib_recv.at[dz],
            device_id=sibling, device_id_type=MESH,
        )

    def z_copy(dz):
        return pltpu.make_async_remote_copy(
            src_ref=keep.at[dz], dst_ref=part.at[dz],
            send_sem=z_send.at[dz], recv_sem=z_recv.at[dz],
            device_id={"tx": 2 * z_partner(dz) + core}, device_id_type=MESH,
        )

    order = list(range(1, nz)) + [0]
    for dz in order:
        ordered(give, dz, 1 - core)
        sib_copy(dz).start()
    for dz in order:
        ordered(keep, dz, core)
    for dz in order:
        sib_copy(dz).wait_recv()
        keep[dz] = keep[dz] + got[dz]
        if dz:
            z_copy(dz).start()
    for dz in range(1, nz):
        z_copy(dz).wait_recv()
    total = keep[0]
    for dz in range(1, nz):
        total = total + part[dz]
    for c in range(2):
        for b in range(block):
            at = (c * block + b) * size_y
            out[0, 0, c, b] = total[at : at + size_y]
    misfit_out[0, 0] = jnp.sum(total[cells_rows : cells_rows + 8])

    for which in range(4):
        each_dir(lambda d, w=which: halo_copy(w, d).wait_send(), to_side)
    each_dir(lambda d: inj_copy(d).wait_send(), to_side)
    for k in range(1, n_gx * n_gy):
        mis_copy(k).wait_send()
    for dz in order:
        sib_copy(dz).wait_send()
    for dz in range(1, nz):
        z_copy(dz).wait_send()


def on_device(sizes, cond_h, cond_v, fwd_init, adj_init, observed, footprint, owner, rec_cells):
    n_tx, n_gx, n_gy = sizes
    nz = n_tx // 2
    size_x, size_y, depth = cond_h.shape
    rows_w = window_rows(n_gx, size_x)
    rows = LOW + rows_w + 1
    wy = size_y + 2 * HALO
    block = size_x // n_tx
    packed = 2 * block * size_y + 8
    f32 = jnp.float32
    n_dirs = len(DIRS)
    plane = n_gx * n_gy
    dma = pltpu.SemaphoreType.DMA
    hbm, vmem, smem = pl.ANY, pltpu.VMEM, pltpu.SMEM
    owned, misfit = pl.pallas_call(
        functools.partial(kernel, sizes),
        out_shape=(
            jax.ShapeDtypeStruct((1, 1, 2, block, size_y, depth), f32),
            jax.ShapeDtypeStruct((1, 1), f32),
        ),
        in_specs=[
            pl.BlockSpec(memory_space=s) for s in (hbm, hbm, hbm, hbm, vmem, smem, smem, vmem)
        ],
        out_specs=(pl.BlockSpec(memory_space=vmem), pl.BlockSpec(memory_space=smem)),
        scratch_shapes=[
            vmem((6, rows, wy, depth), f32),
            vmem((6, rows, wy, depth), f32),
            vmem((2, rows, wy, depth), f32),
            vmem((2, rows, wy, depth), f32),
            vmem((2, rows, wy, depth), f32),
            vmem((STEPS, 3, rows, wy, depth), f32),
            vmem((2, rows, size_y, depth), f32),
            vmem((size_y, depth), f32),
            vmem((9, size_y, depth), f32),
            vmem((3, wy, depth), f32),
            vmem((2 * STEPS, depth), f32),
            vmem((8, depth), f32),
            vmem((plane, 8, depth), f32),
            vmem((nz, packed, depth), f32),
            vmem((nz, packed, depth), f32),
            vmem((nz, packed, depth), f32),
            vmem((nz, packed, depth), f32),
            dma((4,)),
            dma((4, n_dirs)),
            dma((4, n_dirs)),
            dma((n_dirs,)),
            dma((n_dirs,)),
            dma((plane,)),
            dma((plane,)),
            dma((nz,)),
            dma((nz,)),
            dma((nz,)),
            dma((nz,)),
        ],
        compiler_params=pltpu.CompilerParams(
            collective_id=0, has_side_effects=True, vmem_limit_bytes=40 * 1024 * 1024
        ),
    )(cond_h, cond_v, fwd_init, adj_init, observed, footprint, owner, rec_cells)
    return owned, misfit.reshape(())


def solution(mesh):
    placed = (
        P("gx", "gy", None),
        P("gx", "gy", None),
        P("tx", None, "gx", "gy", None),
        P("tx", None, "gx", "gy", None),
        P("tx", None, "gx", "gy", None, None),
        P("tx", "gx", "gy"),
        P("gx", "gy", None),
        P("gx", "gy", None),
    )
    sizes = (mesh.shape["tx"], mesh.shape["gx"], mesh.shape["gy"])
    return jax.shard_map(
        functools.partial(on_device, sizes),
        mesh=mesh,
        in_specs=placed,
        out_specs=(P("gx", "tx", None, None, "gy", None), P()),
        check_vma=False,
    )
```

```python
import functools

import jax
import jax.numpy as jnp
from jax import lax
from jax.experimental import pallas as pl
from jax.experimental.pallas import tpu as pltpu
from jax.sharding import PartitionSpec as P

STEPS = 4
ZREC = 32
STEP_DT = 0.5
HALO = STEPS
LOW = HALO + 1
MESH = pl.DeviceIdType.MESH
DIRS = [(dx, dy) for dx in (-1, 0, 1) for dy in (-1, 0, 1) if (dx, dy) != (0, 0)]


def window_rows(gx_size, size_x):
    return size_x + (HALO if gx_size == 2 else 2 * HALO)


def kernel(
    sizes,
    cond_h, cond_v, fwd, adj, observed_in, footprint_in, owner_in, rec_in,
    out, misfit_out,
    fw, aw, cw, decay, drive, kept, grad, inj_own, inj_in, inj_win, obs_scr,
    observed, footprint, owner, rec_cells,
    mis_own, mis_in, give, keep, got, part,
    loc_sem, halo_send, halo_recv, inj_send, inj_recv, mis_send, mis_recv,
    sib_send, sib_recv, z_send, z_recv,
):
    n_tx, n_gx, n_gy = sizes
    nz = n_tx // 2
    size_x, size_y, depth = cond_h.shape
    rows_w = window_rows(n_gx, size_x)
    wy = size_y + 2 * HALO
    it, ix, iy = lax.axis_index("tx"), lax.axis_index("gx"), lax.axis_index("gy")
    core = lax.rem(it, 2)
    iz = it // 2
    has = {}
    for dx, dy in DIRS:
        ok = None
        for d, i, n in ((dx, ix, n_gx), (dy, iy, n_gy)):
            if d:
                one = (i > 0) if d < 0 else (i < n - 1)
                ok = one if ok is None else jnp.logical_and(ok, one)
        has[(dx, dy)] = ok
    has_lo, has_hi = has[(-1, 0)], has[(1, 0)]
    start = jnp.where(has_lo, -HALO, 0)

    def plane_partner(k):
        ox, oy = k // n_gy, k % n_gy
        return {"gx": lax.rem(ix + ox, n_gx), "gy": lax.rem(iy + oy, n_gy)}

    sibling = {"tx": it + 1 - 2 * core}

    def z_partner(dz):
        return lax.rem(iz + dz, nz)

    tile_x, tile_y = pl.ds(LOW, size_x), pl.ds(0, size_y)
    locals_ = [
        pltpu.make_async_copy(cond_h, cw.at[0, tile_x, tile_y], loc_sem.at[0]),
        pltpu.make_async_copy(cond_v, cw.at[1, tile_x, tile_y], loc_sem.at[1]),
        pltpu.make_async_copy(fwd.at[0], fw.at[:, tile_x, tile_y], loc_sem.at[2]),
        pltpu.make_async_copy(adj.at[0], aw.at[:, tile_x, tile_y], loc_sem.at[3]),
        pltpu.make_async_copy(observed_in, observed, loc_sem.at[4]),
        pltpu.make_async_copy(rec_in, rec_cells, loc_sem.at[5]),
        pltpu.make_async_copy(footprint_in, footprint, loc_sem.at[6]),
        pltpu.make_async_copy(owner_in, owner, loc_sem.at[7]),
    ]
    for c in locals_:
        c.start()

    rows_all = fw.shape[1]
    top = LOW + size_x
    for ref in (cw, fw, aw):
        comps = ref.shape[0]
        ref[:, :, size_y:wy] = jnp.zeros((comps, rows_all, wy - size_y, depth), jnp.float32)
        if ref is cw and n_gx == 2:
            continue
        zero_rows = (LOW - 1, top) if n_gx == 2 else (*range(LOW), *range(top, rows_all))
        for r in zero_rows:
            ref[:, r, 0:size_y] = jnp.zeros((comps, size_y, depth), jnp.float32)
    inj_in[...] = jnp.zeros_like(inj_in)

    barrier = pltpu.get_barrier_semaphore()
    for k in range(1, n_gx * n_gy):
        pl.semaphore_signal(barrier, inc=1, device_id=plane_partner(k), device_id_type=MESH)
    pl.semaphore_signal(barrier, inc=1, device_id=sibling, device_id_type=MESH)
    for dz in range(1, nz):
        pl.semaphore_signal(
            barrier, inc=1, device_id={"tx": 2 * z_partner(dz) + core}, device_id_type=MESH
        )
    pl.semaphore_wait(barrier, n_gx * n_gy - 1 + 1 + nz - 1)

    def source(d, size, deep=HALO):
        return pl.ds(0, size) if d == 0 else (pl.ds(size - deep, deep) if d > 0 else pl.ds(0, deep))

    def target_x(d, deep=HALO):
        return tile_x if d == 0 else (pl.ds(LOW - deep, deep) if d > 0 else pl.ds(LOW + size_x, deep))

    def target_y(d):
        return tile_y if d == 0 else (pl.ds(size_y + HALO, HALO) if d > 0 else pl.ds(size_y, HALO))

    def halo_copy(which, d):
        dx, dy = DIRS[d]
        sx, sy = source(dx, size_x), source(dy, size_y)
        tx_, ty_ = target_x(dx), target_y(dy)
        if which < 2:
            sx, tx_ = source(dx, size_x, HALO - 1), target_x(dx, HALO - 1)
        src, dst = {
            0: (cond_h.at[sx, sy], cw.at[0, tx_, ty_]),
            1: (cond_v.at[sx, sy], cw.at[1, tx_, ty_]),
            2: (fwd.at[0, :, sx, sy], fw.at[:, tx_, ty_]),
            3: (adj.at[0, :, sx, sy], aw.at[:, tx_, ty_]),
        }[which]
        return pltpu.make_async_remote_copy(
            src_ref=src, dst_ref=dst,
            send_sem=halo_send.at[which, d], recv_sem=halo_recv.at[which, d],
            device_id={"gx": ix + dx, "gy": iy + dy}, device_id_type=MESH,
        )

    def each_dir(fn, conds):
        for d, (dx, dy) in enumerate(DIRS):
            if (dx and n_gx == 1) or (dy and n_gy == 1):
                continue
            pl.when(conds(dx, dy))(functools.partial(fn, d))

    def to_side(dx, dy):
        return has[(dx, dy)]

    def from_side(dx, dy):
        return has[(-dx, -dy)]

    for which in range(3):
        each_dir(lambda d, w=which: halo_copy(w, d).start(), to_side)

    lanes = lax.broadcasted_iota(jnp.int32, (size_y, depth), 1)
    for c in locals_[4:]:
        c.wait()
    highest = lax.Precision.HIGHEST
    rpt = rec_cells.shape[-1]
    cells = rec_cells[0]
    in_y = (lax.broadcasted_iota(jnp.int32, (size_y, rpt), 0) == cells % size_y).astype(jnp.float32)
    in_x = (lax.broadcasted_iota(jnp.int32, (size_x, rpt), 0) == cells // size_y).astype(jnp.float32)
    lane_x = (
        lax.broadcasted_iota(jnp.int32, (size_x, depth), 0)
        == lax.broadcasted_iota(jnp.int32, (size_x, depth), 1) % size_x
    ).astype(jnp.float32)
    lane_k = (
        lax.broadcasted_iota(jnp.int32, (2 * STEPS, depth), 0)
        == lax.broadcasted_iota(jnp.int32, (2 * STEPS, depth), 1) // size_x
    ).astype(jnp.float32)
    for n in range(STEPS):
        obs_scr[2 * n : 2 * n + 2, 0:rpt] = observed[0, n, 0, 0]
    over0 = (((0,), (0,)), ((), ()))
    at_x = lax.dot_general(in_x, lane_x, over0, precision=highest, preferred_element_type=jnp.float32)
    obs_l = at_x * lax.dot_general(
        obs_scr[:, 0:rpt], lane_k, over0, precision=highest, preferred_element_type=jnp.float32
    )
    count = jnp.dot(in_y, at_x, precision=highest, preferred_element_type=jnp.float32)
    obs_sum = jnp.dot(in_y, obs_l, precision=highest, preferred_element_type=jnp.float32)

    for n in range(STEPS):
        for x in sorted({size_x, size_x + HALO, rows_w}):
            kept[n, :, LOW + x] = jnp.zeros((3, wy, depth), jnp.float32)

    def wait_in(which):
        locals_[which].wait()
        each_dir(lambda d: halo_copy(which, d).wait_recv(), from_side)

    wait_in(0)
    wait_in(1)
    sub = lax.broadcasted_iota(jnp.int32, (wy, depth), 0)
    lane = lax.broadcasted_iota(jnp.int32, (wy, depth), 1)
    y_hi = jnp.where(has[(0, 1)], 1.0, 0.0)
    y_lo = jnp.where(has[(0, -1)], 1.0, 0.0)
    y_ok = jnp.where(sub < size_y, 1.0, jnp.where(sub < size_y + HALO, y_hi, y_lo))
    half = STEP_DT * y_ok

    def span(j):
        if n_gx == 2:
            rows = rows_w - j + j % 2
            return jnp.where(has_lo, j - HALO, 0), rows // 2, 2
        return start, 8, rows_w // 8


    def coefficients(k, carry):
        for i in range(rows_w // 4):
            x = start + k * (rows_w // 4) + i
            ok = y_ok * jnp.where(jnp.logical_or(x < size_x, has_hi), 1.0, 0.0)
            for c in range(2):
                rate = 0.25 * cw[c, x + LOW]
                scaled = ok / (1.0 + rate)
                drive[c, x + LOW] = STEP_DT * scaled
                decay[c, x + LOW] = (1.0 - rate) * scaled
        return carry

    lax.fori_loop(0, 4, coefficients, 0)

    def y_next(f):
        return pltpu.roll(f, wy - 1, 0)

    def y_prev(f):
        return pltpu.roll(f, 1, 0)

    def z_next(f):
        return jnp.where(lane == depth - 1, 0.0, pltpu.roll(f, depth - 1, 1))

    def z_prev(f):
        return jnp.where(lane == 0, 0.0, pltpu.roll(f, 1, 1))

    def step_rows(r, chunk, e_src, h, e_dst, after):
        ex, ey, ez = (e_src[c, r] for c in range(3))
        hp_y, hp_z = h[1, r - 1], h[2, r - 1]
        for i in range(chunk):
            ey_n, ez_n = e_src[1, r + i + 1], e_src[2, r + i + 1]
            ex_n = e_src[0, r + i + 1] if i < chunk - 1 else None
            hx = h[0, r + i] - half * ((y_next(ez) - ez) - (z_next(ey) - ey))
            hy = h[1, r + i] - half * ((z_next(ex) - ex) - (ez_n - ez))
            hz = h[2, r + i] - half * ((ey_n - ey) - (y_next(ex) - ex))
            h[0, r + i] = hx
            h[1, r + i] = hy
            h[2, r + i] = hz
            cx = (hz - y_prev(hz)) - (hy - z_prev(hy))
            cy = (hx - z_prev(hx)) - (hz - hp_z)
            cz = (hy - hp_y) - (hx - y_prev(hx))
            hp_y, hp_z = hy, hz
            dec_h, drv_h = decay[0, r + i], drive[0, r + i]
            dec_v, drv_v = decay[1, r + i], drive[1, r + i]
            new = (dec_h * ex + drv_h * cx, dec_h * ey + drv_h * cy, dec_v * ez + drv_v * cz)
            for c in range(3):
                e_dst[c, r + i] = new[c]
            if after is not None:
                after(r + i, new)
            ex, ey, ez = ex_n, ey_n, ez_n

    def step(j, e_src, h, e_dst, after=None):
        first, chunk, chunks = span(j)

        def body(k, carry):
            step_rows(first + LOW + k * chunk, chunk, e_src, h, e_dst, after)
            return carry

        lax.fori_loop(0, chunks, body, 0)

    wait_in(2)
    each_dir(lambda d: halo_copy(3, d).start(), to_side)
    for n in range(STEPS):
        step(n, fw.at[0:3] if n == 0 else kept.at[n - 1], fw.at[3:6], kept.at[n])

    rec = jnp.zeros((size_y, depth), jnp.float32)
    for n in range(STEPS):
        for c in range(2):
            for x in range(size_x):
                at = (2 * n + c) * size_x + x
                e = kept[n, c, LOW + x, 0:size_y]
                rec = jnp.where(lanes == at, pltpu.roll(e, (at - ZREC) % depth, 1), rec)
    inj_own[...] = count * rec - obs_sum

    def inj_copy(d):
        dx, dy = DIRS[d]
        return pltpu.make_async_remote_copy(
            src_ref=inj_own, dst_ref=inj_in.at[(1 - dx) * 3 + 1 - dy],
            send_sem=inj_send.at[d], recv_sem=inj_recv.at[d],
            device_id={"gx": ix + dx, "gy": iy + dy}, device_id_type=MESH,
        )

    each_dir(lambda d: inj_copy(d).start(), to_side)

    at_rec = lax.dot_general(in_y, rec, over0, precision=highest, preferred_element_type=jnp.float32)
    resid = at_x * at_rec - obs_l
    mis_own[...] = 0.5 * jnp.sum((resid * resid).reshape(rpt // 8, 8, depth), axis=0)

    def mis_copy(k):
        return pltpu.make_async_remote_copy(
            src_ref=mis_own, dst_ref=mis_in.at[k],
            send_sem=mis_send.at[k], recv_sem=mis_recv.at[k],
            device_id=plane_partner(k), device_id_type=MESH,
        )

    for k in range(1, n_gx * n_gy):
        mis_copy(k).start()

    wait_in(3)
    each_dir(lambda d: inj_copy(d).wait_recv(), from_side)
    sub8 = lax.broadcasted_iota(jnp.int32, (2 * HALO, depth), 0)
    for q in range(3):
        own = inj_own[...] if q == 1 else inj_in[q * 3 + 1]
        inj_win[q, 0:size_y] = own
        inj_win[q, size_y:wy] = jnp.where(
            sub8 < HALO,
            inj_in[q * 3 + 2, 0 : 2 * HALO],
            inj_in[q * 3, size_y - 2 * HALO : size_y],
        )

    for n in reversed(range(STEPS)):
        first, chunk, chunks = span(STEPS - 1 - n)

        def inject(k, carry, n=n, first=first, chunk=chunk):
            for i in range(chunk):
                x = first + k * chunk + i
                plane = inj_win[(x + size_x) // size_x]
                for c in range(2):
                    at = (2 * n + c) * size_x + lax.rem(x + size_x, size_x)
                    moved = pltpu.roll(plane, lax.rem(ZREC + depth - at, depth), 1)
                    aw[c, x + LOW] = aw[c, x + LOW] + jnp.where(lane == ZREC, moved, 0.0)
            return carry

        lax.fori_loop(0, chunks, inject, 0)

        def add_gradient(r, new, n=n):
            tile = slice(0, size_y)
            g_h = new[0][tile] * kept[n, 0, r, tile] + new[1][tile] * kept[n, 1, r, tile]
            g_v = new[2][tile] * kept[n, 2, r, tile]
            if n < STEPS - 1:
                g_h = grad[0, r] + g_h
                g_v = grad[1, r] + g_v
            grad[0, r] = g_h
            grad[1, r] = g_v

        step(STEPS - 1 - n, aw.at[0:3], aw.at[3:6], aw.at[0:3], add_gradient)

    for k in range(1, n_gx * n_gy):
        mis_copy(k).wait_recv()
    misfit = mis_own[...]
    for k in range(1, n_gx * n_gy):
        misfit = misfit + mis_in[k]

    flag = footprint[0, 0, 0].astype(jnp.float32)
    block = size_x // n_tx
    cells_rows = 2 * block * size_y

    def ordered(dst, dz, to_core):
        z = z_partner(dz)
        first = owner[0, 0, 2 * z + to_core] * block
        for c in range(2):
            for b in range(block):
                at = (c * block + b) * size_y
                dst[dz, at : at + size_y] = flag * grad[c, LOW + first + b]
        dst[dz, cells_rows : cells_rows + 8] = misfit

    def sib_copy(dz):
        return pltpu.make_async_remote_copy(
            src_ref=give.at[dz], dst_ref=got.at[dz],
            send_sem=sib_send.at[dz], recv_sem=sib_recv.at[dz],
            device_id=sibling, device_id_type=MESH,
        )

    def z_copy(dz):
        return pltpu.make_async_remote_copy(
            src_ref=keep.at[dz], dst_ref=part.at[dz],
            send_sem=z_send.at[dz], recv_sem=z_recv.at[dz],
            device_id={"tx": 2 * z_partner(dz) + core}, device_id_type=MESH,
        )

    order = list(range(1, nz)) + [0]
    for dz in order:
        ordered(give, dz, 1 - core)
        sib_copy(dz).start()
    for dz in order:
        ordered(keep, dz, core)
    for dz in order:
        sib_copy(dz).wait_recv()
        keep[dz] = keep[dz] + got[dz]
        if dz:
            z_copy(dz).start()
    for dz in range(1, nz):
        z_copy(dz).wait_recv()
    total = keep[0]
    for dz in range(1, nz):
        total = total + part[dz]
    for c in range(2):
        for b in range(block):
            at = (c * block + b) * size_y
            out[0, 0, c, b] = total[at : at + size_y]
    misfit_out[0, 0] = jnp.sum(total[cells_rows : cells_rows + 8])

    for which in range(4):
        each_dir(lambda d, w=which: halo_copy(w, d).wait_send(), to_side)
    each_dir(lambda d: inj_copy(d).wait_send(), to_side)
    for k in range(1, n_gx * n_gy):
        mis_copy(k).wait_send()
    for dz in order:
        sib_copy(dz).wait_send()
    for dz in range(1, nz):
        z_copy(dz).wait_send()


def on_device(sizes, cond_h, cond_v, fwd_init, adj_init, observed, footprint, owner, rec_cells):
    n_tx, n_gx, n_gy = sizes
    nz = n_tx // 2
    size_x, size_y, depth = cond_h.shape
    rows_w = window_rows(n_gx, size_x)
    rows = LOW + rows_w + 1
    wy = size_y + 2 * HALO
    block = size_x // n_tx
    packed = 2 * block * size_y + 8
    f32 = jnp.float32
    n_dirs = len(DIRS)
    plane = n_gx * n_gy
    dma = pltpu.SemaphoreType.DMA
    hbm, vmem, smem = pl.ANY, pltpu.VMEM, pltpu.SMEM
    owned, misfit = pl.pallas_call(
        functools.partial(kernel, sizes),
        out_shape=(
            jax.ShapeDtypeStruct((1, 1, 2, block, size_y, depth), f32),
            jax.ShapeDtypeStruct((1, 1), f32),
        ),
        in_specs=[
            pl.BlockSpec(memory_space=s) for s in [hbm] * 8
        ],
        out_specs=(pl.BlockSpec(memory_space=vmem), pl.BlockSpec(memory_space=smem)),
        scratch_shapes=[
            vmem((6, rows, wy, depth), f32),
            vmem((6, rows, wy, depth), f32),
            vmem((2, rows, wy, depth), f32),
            vmem((2, rows, wy, depth), f32),
            vmem((2, rows, wy, depth), f32),
            vmem((STEPS, 3, rows, wy, depth), f32),
            vmem((2, rows, size_y, depth), f32),
            vmem((size_y, depth), f32),
            vmem((9, size_y, depth), f32),
            vmem((3, wy, depth), f32),
            vmem((2 * STEPS, depth), f32),
            vmem(observed.shape, f32),
            smem(footprint.shape, jnp.int32),
            smem(owner.shape, jnp.int32),
            vmem(rec_cells.shape, jnp.int32),
            vmem((8, depth), f32),
            vmem((plane, 8, depth), f32),
            vmem((nz, packed, depth), f32),
            vmem((nz, packed, depth), f32),
            vmem((nz, packed, depth), f32),
            vmem((nz, packed, depth), f32),
            dma((8,)),
            dma((4, n_dirs)),
            dma((4, n_dirs)),
            dma((n_dirs,)),
            dma((n_dirs,)),
            dma((plane,)),
            dma((plane,)),
            dma((nz,)),
            dma((nz,)),
            dma((nz,)),
            dma((nz,)),
        ],
        compiler_params=pltpu.CompilerParams(
            collective_id=0, has_side_effects=True, vmem_limit_bytes=60 * 1024 * 1024
        ),
    )(cond_h, cond_v, fwd_init, adj_init, observed, footprint, owner, rec_cells)
    return owned, misfit.reshape(())


def solution(mesh):
    placed = (
        P("gx", "gy", None),
        P("gx", "gy", None),
        P("tx", None, "gx", "gy", None),
        P("tx", None, "gx", "gy", None),
        P("tx", None, "gx", "gy", None, None),
        P("tx", "gx", "gy"),
        P("gx", "gy", None),
        P("gx", "gy", None),
    )
    sizes = (mesh.shape["tx"], mesh.shape["gx"], mesh.shape["gy"])
    return jax.shard_map(
        functools.partial(on_device, sizes),
        mesh=mesh,
        in_specs=placed,
        out_specs=(P("gx", "tx", None, None, "gy", None), P()),
        check_vma=False,
    )
```

```python
import functools

import jax
import jax.numpy as jnp
from jax import lax
from jax.experimental import pallas as pl
from jax.experimental.pallas import tpu as pltpu
from jax.sharding import PartitionSpec as P

STEPS = 4
ZREC = 32
STEP_DT = 0.5
HALO = STEPS
LOW = HALO + 1
MESH = pl.DeviceIdType.MESH
DIRS = [(dx, dy) for dx in (-1, 0, 1) for dy in (-1, 0, 1) if (dx, dy) != (0, 0)]


def window_rows(gx_size, size_x):
    return size_x + (HALO if gx_size == 2 else 2 * HALO)


def kernel(
    sizes,
    cond_h, cond_v, fwd, adj, observed_in, footprint_in, owner_in, rec_in,
    out, misfit_out,
    fw, aw, cw, decay, drive, kept, grad, inj_own, inj_in, inj_win, obs_scr,
    observed, footprint, owner, rec_cells,
    mis_own, mis_in, mis_tiles, mis_got, mis_chip, mis_part, give, keep, got, part,
    loc_sem, halo_send, halo_recv, inj_send, inj_recv, mis_send, mis_recv,
    mis_sib_sem, mis_z_send, mis_z_recv,
    sib_send, sib_recv, z_send, z_recv,
):
    n_tx, n_gx, n_gy = sizes
    nz = n_tx // 2
    size_x, size_y, depth = cond_h.shape
    rows_w = window_rows(n_gx, size_x)
    wy = size_y + 2 * HALO
    it, ix, iy = lax.axis_index("tx"), lax.axis_index("gx"), lax.axis_index("gy")
    core = lax.rem(it, 2)
    iz = it // 2
    has = {}
    for dx, dy in DIRS:
        ok = None
        for d, i, n in ((dx, ix, n_gx), (dy, iy, n_gy)):
            if d:
                one = (i > 0) if d < 0 else (i < n - 1)
                ok = one if ok is None else jnp.logical_and(ok, one)
        has[(dx, dy)] = ok
    has_lo, has_hi = has[(-1, 0)], has[(1, 0)]
    start = jnp.where(has_lo, -HALO, 0)

    def plane_partner(k):
        ox, oy = k // n_gy, k % n_gy
        return {"gx": lax.rem(ix + ox, n_gx), "gy": lax.rem(iy + oy, n_gy)}

    sibling = {"tx": it + 1 - 2 * core}

    def z_partner(dz):
        return lax.rem(iz + dz, nz)

    tile_x, tile_y = pl.ds(LOW, size_x), pl.ds(0, size_y)
    locals_ = [
        pltpu.make_async_copy(cond_h, cw.at[0, tile_x, tile_y], loc_sem.at[0]),
        pltpu.make_async_copy(cond_v, cw.at[1, tile_x, tile_y], loc_sem.at[1]),
        pltpu.make_async_copy(fwd.at[0], fw.at[:, tile_x, tile_y], loc_sem.at[2]),
        pltpu.make_async_copy(adj.at[0], aw.at[:, tile_x, tile_y], loc_sem.at[3]),
        pltpu.make_async_copy(observed_in, observed, loc_sem.at[4]),
        pltpu.make_async_copy(rec_in, rec_cells, loc_sem.at[5]),
        pltpu.make_async_copy(footprint_in, footprint, loc_sem.at[6]),
        pltpu.make_async_copy(owner_in, owner, loc_sem.at[7]),
    ]
    for c in locals_:
        c.start()

    rows_all = fw.shape[1]
    top = LOW + size_x
    for ref in (cw, fw, aw):
        comps = ref.shape[0]
        ref[:, :, size_y:wy] = jnp.zeros((comps, rows_all, wy - size_y, depth), jnp.float32)
        if ref is cw and n_gx == 2:
            continue
        zero_rows = (LOW - 1, top) if n_gx == 2 else (*range(LOW), *range(top, rows_all))
        for r in zero_rows:
            ref[:, r, 0:size_y] = jnp.zeros((comps, size_y, depth), jnp.float32)
    inj_in[...] = jnp.zeros_like(inj_in)

    barrier = pltpu.get_barrier_semaphore()
    for k in range(1, n_gx * n_gy):
        pl.semaphore_signal(barrier, inc=1, device_id=plane_partner(k), device_id_type=MESH)
    pl.semaphore_signal(barrier, inc=1, device_id=sibling, device_id_type=MESH)
    for dz in range(1, nz):
        pl.semaphore_signal(
            barrier, inc=1, device_id={"tx": 2 * z_partner(dz) + core}, device_id_type=MESH
        )
    pl.semaphore_wait(barrier, n_gx * n_gy - 1 + 1 + nz - 1)

    def source(d, size, deep=HALO):
        return pl.ds(0, size) if d == 0 else (pl.ds(size - deep, deep) if d > 0 else pl.ds(0, deep))

    def target_x(d, deep=HALO):
        return tile_x if d == 0 else (pl.ds(LOW - deep, deep) if d > 0 else pl.ds(LOW + size_x, deep))

    def target_y(d):
        return tile_y if d == 0 else (pl.ds(size_y + HALO, HALO) if d > 0 else pl.ds(size_y, HALO))

    def halo_copy(which, d):
        dx, dy = DIRS[d]
        sx, sy = source(dx, size_x), source(dy, size_y)
        tx_, ty_ = target_x(dx), target_y(dy)
        if which < 2:
            sx, tx_ = source(dx, size_x, HALO - 1), target_x(dx, HALO - 1)
        src, dst = {
            0: (cond_h.at[sx, sy], cw.at[0, tx_, ty_]),
            1: (cond_v.at[sx, sy], cw.at[1, tx_, ty_]),
            2: (fwd.at[0, :, sx, sy], fw.at[:, tx_, ty_]),
            3: (adj.at[0, :, sx, sy], aw.at[:, tx_, ty_]),
        }[which]
        return pltpu.make_async_remote_copy(
            src_ref=src, dst_ref=dst,
            send_sem=halo_send.at[which, d], recv_sem=halo_recv.at[which, d],
            device_id={"gx": ix + dx, "gy": iy + dy}, device_id_type=MESH,
        )

    def each_dir(fn, conds):
        for d, (dx, dy) in enumerate(DIRS):
            if (dx and n_gx == 1) or (dy and n_gy == 1):
                continue
            pl.when(conds(dx, dy))(functools.partial(fn, d))

    def to_side(dx, dy):
        return has[(dx, dy)]

    def from_side(dx, dy):
        return has[(-dx, -dy)]

    for which in range(3):
        each_dir(lambda d, w=which: halo_copy(w, d).start(), to_side)

    lanes = lax.broadcasted_iota(jnp.int32, (size_y, depth), 1)
    for c in locals_[4:]:
        c.wait()
    highest = lax.Precision.HIGHEST
    rpt = rec_cells.shape[-1]
    cells = rec_cells[0]
    in_y = (lax.broadcasted_iota(jnp.int32, (size_y, rpt), 0) == cells % size_y).astype(jnp.float32)
    in_x = (lax.broadcasted_iota(jnp.int32, (size_x, rpt), 0) == cells // size_y).astype(jnp.float32)
    lane_x = (
        lax.broadcasted_iota(jnp.int32, (size_x, depth), 0)
        == lax.broadcasted_iota(jnp.int32, (size_x, depth), 1) % size_x
    ).astype(jnp.float32)
    lane_k = (
        lax.broadcasted_iota(jnp.int32, (2 * STEPS, depth), 0)
        == lax.broadcasted_iota(jnp.int32, (2 * STEPS, depth), 1) // size_x
    ).astype(jnp.float32)
    for n in range(STEPS):
        obs_scr[2 * n : 2 * n + 2, 0:rpt] = observed[0, n, 0, 0]
    over0 = (((0,), (0,)), ((), ()))
    at_x = lax.dot_general(in_x, lane_x, over0, precision=highest, preferred_element_type=jnp.float32)
    obs_l = at_x * lax.dot_general(
        obs_scr[:, 0:rpt], lane_k, over0, precision=highest, preferred_element_type=jnp.float32
    )
    count = jnp.dot(in_y, at_x, precision=highest, preferred_element_type=jnp.float32)
    obs_sum = jnp.dot(in_y, obs_l, precision=highest, preferred_element_type=jnp.float32)

    for n in range(STEPS):
        for x in sorted({size_x, size_x + HALO, rows_w}):
            kept[n, :, LOW + x] = jnp.zeros((3, wy, depth), jnp.float32)

    def wait_in(which):
        locals_[which].wait()
        each_dir(lambda d: halo_copy(which, d).wait_recv(), from_side)

    wait_in(0)
    wait_in(1)
    sub = lax.broadcasted_iota(jnp.int32, (wy, depth), 0)
    lane = lax.broadcasted_iota(jnp.int32, (wy, depth), 1)
    y_hi = jnp.where(has[(0, 1)], 1.0, 0.0)
    y_lo = jnp.where(has[(0, -1)], 1.0, 0.0)
    y_ok = jnp.where(sub < size_y, 1.0, jnp.where(sub < size_y + HALO, y_hi, y_lo))
    half = STEP_DT * y_ok

    def span(j):
        if n_gx == 2:
            return jnp.where(has_lo, j - HALO, 0), rows_w - j, 1
        return start, 8, rows_w // 8


    def coefficients(k, carry):
        for i in range(rows_w // 4):
            x = start + k * (rows_w // 4) + i
            ok = y_ok * jnp.where(jnp.logical_or(x < size_x, has_hi), 1.0, 0.0)
            for c in range(2):
                rate = 0.25 * cw[c, x + LOW]
                scaled = ok / (1.0 + rate)
                drive[c, x + LOW] = STEP_DT * scaled
                decay[c, x + LOW] = (1.0 - rate) * scaled
        return carry

    lax.fori_loop(0, 4, coefficients, 0)

    def y_next(f):
        return pltpu.roll(f, wy - 1, 0)

    def y_prev(f):
        return pltpu.roll(f, 1, 0)

    def z_next(f):
        return jnp.where(lane == depth - 1, 0.0, pltpu.roll(f, depth - 1, 1))

    def z_prev(f):
        return jnp.where(lane == 0, 0.0, pltpu.roll(f, 1, 1))

    def step_rows(r, chunk, load, h, e_dst, after, keep_h):
        ex, ey, ez = (load(c, r) for c in range(3))
        hp_y, hp_z = h[1, r - 1], h[2, r - 1]
        for i in range(chunk):
            ey_n, ez_n = load(1, r + i + 1), load(2, r + i + 1)
            ex_n = load(0, r + i + 1) if i < chunk - 1 else None
            hx = h[0, r + i] - half * ((y_next(ez) - ez) - (z_next(ey) - ey))
            hy = h[1, r + i] - half * ((z_next(ex) - ex) - (ez_n - ez))
            hz = h[2, r + i] - half * ((ey_n - ey) - (y_next(ex) - ex))
            if keep_h:
                h[0, r + i] = hx
                h[1, r + i] = hy
                h[2, r + i] = hz
            cx = (hz - y_prev(hz)) - (hy - z_prev(hy))
            cy = (hx - z_prev(hx)) - (hz - hp_z)
            cz = (hy - hp_y) - (hx - y_prev(hx))
            hp_y, hp_z = hy, hz
            dec_h, drv_h = decay[0, r + i], drive[0, r + i]
            dec_v, drv_v = decay[1, r + i], drive[1, r + i]
            new = (dec_h * ex + drv_h * cx, dec_h * ey + drv_h * cy, dec_v * ez + drv_v * cz)
            for c in range(3):
                e_dst[c, r + i] = new[c]
            if after is not None:
                after(r + i, new)
            ex, ey, ez = ex_n, ey_n, ez_n

    def step(j, load, h, e_dst, after=None):
        first, chunk, chunks = span(j)

        def body(k, carry):
            keep_h = j < STEPS - 1 or chunks > 1
            step_rows(first + LOW + k * chunk, chunk, load, h, e_dst, after, keep_h)
            return carry

        if chunks == 1:
            body(0, 0)
        else:
            lax.fori_loop(0, chunks, body, 0)

    wait_in(2)
    each_dir(lambda d: halo_copy(3, d).start(), to_side)
    for n in range(STEPS):
        e_src = fw if n == 0 else kept.at[n - 1]
        step(n, lambda c, r, e=e_src: e[c, r], fw.at[3:6], kept.at[n])

    rec = jnp.zeros((size_y, depth), jnp.float32)
    for n in range(STEPS):
        for c in range(2):
            for x in range(size_x):
                at = (2 * n + c) * size_x + x
                e = kept[n, c, LOW + x, 0:size_y]
                rec = jnp.where(lanes == at, pltpu.roll(e, (at - ZREC) % depth, 1), rec)
    inj_own[...] = count * rec - obs_sum

    def inj_copy(d):
        dx, dy = DIRS[d]
        return pltpu.make_async_remote_copy(
            src_ref=inj_own, dst_ref=inj_in.at[(1 - dx) * 3 + 1 - dy],
            send_sem=inj_send.at[d], recv_sem=inj_recv.at[d],
            device_id={"gx": ix + dx, "gy": iy + dy}, device_id_type=MESH,
        )

    each_dir(lambda d: inj_copy(d).start(), to_side)

    at_rec = lax.dot_general(in_y, rec, over0, precision=highest, preferred_element_type=jnp.float32)
    resid = at_x * at_rec - obs_l
    mis_own[...] = 0.5 * jnp.sum((resid * resid).reshape(rpt // 8, 8, depth), axis=0)

    def mis_copy(k):
        return pltpu.make_async_remote_copy(
            src_ref=mis_own, dst_ref=mis_in.at[k],
            send_sem=mis_send.at[k], recv_sem=mis_recv.at[k],
            device_id=plane_partner(k), device_id_type=MESH,
        )

    for k in range(1, n_gx * n_gy):
        mis_copy(k).start()

    wait_in(3)
    each_dir(lambda d: inj_copy(d).wait_recv(), from_side)
    sub8 = lax.broadcasted_iota(jnp.int32, (2 * HALO, depth), 0)
    for q in range(3):
        own = inj_own[...] if q == 1 else inj_in[q * 3 + 1]
        inj_win[q, 0:size_y] = own
        inj_win[q, size_y:wy] = jnp.where(
            sub8 < HALO,
            inj_in[q * 3 + 2, 0 : 2 * HALO],
            inj_in[q * 3, size_y - 2 * HALO : size_y],
        )

    def mis_sib():
        return pltpu.make_async_remote_copy(
            src_ref=mis_tiles, dst_ref=mis_got,
            send_sem=mis_sib_sem.at[0], recv_sem=mis_sib_sem.at[1],
            device_id=sibling, device_id_type=MESH,
        )

    def mis_z(dz):
        return pltpu.make_async_remote_copy(
            src_ref=mis_chip, dst_ref=mis_part.at[dz],
            send_sem=mis_z_send.at[dz], recv_sem=mis_z_recv.at[dz],
            device_id={"tx": 2 * z_partner(dz) + core}, device_id_type=MESH,
        )

    def misfit_round(n):
        if n == STEPS - 1:
            total = mis_own[...]
            for k in range(1, n_gx * n_gy):
                mis_copy(k).wait_recv()
                total = total + mis_in[k]
            mis_tiles[...] = total
            mis_sib().start()
        elif n == STEPS - 2:
            mis_sib().wait_recv()
            mis_chip[...] = mis_tiles[...] + mis_got[...]
            for dz in range(1, nz):
                mis_z(dz).start()
        elif n == STEPS - 3:
            total = mis_chip[...]
            for dz in range(1, nz):
                mis_z(dz).wait_recv()
                total = total + mis_part[dz]
            misfit_out[0, 0] = jnp.sum(total)

    for n in reversed(range(STEPS)):
        def load(c, r, n=n):
            e = aw[c, r]
            if c == 2:
                return e
            x = r - LOW + size_x
            at = (2 * n + c) * size_x + lax.rem(x, size_x)
            moved = pltpu.roll(inj_win[x // size_x], lax.rem(ZREC + depth - at, depth), 1)
            return e + jnp.where(lane == ZREC, moved, 0.0)

        def add_gradient(r, new, n=n):
            tile = slice(0, size_y)
            g_h = new[0][tile] * kept[n, 0, r, tile] + new[1][tile] * kept[n, 1, r, tile]
            g_v = new[2][tile] * kept[n, 2, r, tile]
            if n < STEPS - 1:
                g_h = grad[0, r] + g_h
                g_v = grad[1, r] + g_v
            grad[0, r] = g_h
            grad[1, r] = g_v

        step(STEPS - 1 - n, load, aw.at[3:6], aw.at[0:3], add_gradient)
        misfit_round(n)

    flag = footprint[0, 0, 0].astype(jnp.float32)
    block = size_x // n_tx

    def ordered(dst, dz, to_core):
        z = z_partner(dz)
        first = owner[0, 0, 2 * z + to_core] * block
        for c in range(2):
            for b in range(block):
                at = (c * block + b) * size_y
                dst[dz, at : at + size_y] = flag * grad[c, LOW + first + b]

    def sib_copy(dz):
        return pltpu.make_async_remote_copy(
            src_ref=give.at[dz], dst_ref=got.at[dz],
            send_sem=sib_send.at[dz], recv_sem=sib_recv.at[dz],
            device_id=sibling, device_id_type=MESH,
        )

    def z_copy(dz):
        return pltpu.make_async_remote_copy(
            src_ref=keep.at[dz], dst_ref=part.at[dz],
            send_sem=z_send.at[dz], recv_sem=z_recv.at[dz],
            device_id={"tx": 2 * z_partner(dz) + core}, device_id_type=MESH,
        )

    order = list(range(1, nz)) + [0]
    for dz in order:
        ordered(give, dz, 1 - core)
        sib_copy(dz).start()
    for dz in order:
        ordered(keep, dz, core)
    for dz in order:
        sib_copy(dz).wait_recv()
        keep[dz] = keep[dz] + got[dz]
        if dz:
            z_copy(dz).start()
    for dz in range(1, nz):
        z_copy(dz).wait_recv()
    total = keep[0]
    for dz in range(1, nz):
        total = total + part[dz]
    for c in range(2):
        for b in range(block):
            at = (c * block + b) * size_y
            out[0, 0, c, b] = total[at : at + size_y]

    for which in range(4):
        each_dir(lambda d, w=which: halo_copy(w, d).wait_send(), to_side)
    each_dir(lambda d: inj_copy(d).wait_send(), to_side)
    for k in range(1, n_gx * n_gy):
        mis_copy(k).wait_send()
    mis_sib().wait_send()
    for dz in range(1, nz):
        mis_z(dz).wait_send()
    for dz in order:
        sib_copy(dz).wait_send()
    for dz in range(1, nz):
        z_copy(dz).wait_send()


def on_device(sizes, cond_h, cond_v, fwd_init, adj_init, observed, footprint, owner, rec_cells):
    n_tx, n_gx, n_gy = sizes
    nz = n_tx // 2
    size_x, size_y, depth = cond_h.shape
    rows_w = window_rows(n_gx, size_x)
    rows = LOW + rows_w + 1
    wy = size_y + 2 * HALO
    block = size_x // n_tx
    packed = 2 * block * size_y
    f32 = jnp.float32
    n_dirs = len(DIRS)
    plane = n_gx * n_gy
    dma = pltpu.SemaphoreType.DMA
    hbm, vmem, smem = pl.ANY, pltpu.VMEM, pltpu.SMEM
    owned, misfit = pl.pallas_call(
        functools.partial(kernel, sizes),
        out_shape=(
            jax.ShapeDtypeStruct((1, 1, 2, block, size_y, depth), f32),
            jax.ShapeDtypeStruct((1, 1), f32),
        ),
        in_specs=[
            pl.BlockSpec(memory_space=s) for s in [hbm] * 8
        ],
        out_specs=(pl.BlockSpec(memory_space=vmem), pl.BlockSpec(memory_space=smem)),
        scratch_shapes=[
            vmem((6, rows, wy, depth), f32),
            vmem((6, rows, wy, depth), f32),
            vmem((2, rows, wy, depth), f32),
            vmem((2, rows, wy, depth), f32),
            vmem((2, rows, wy, depth), f32),
            vmem((STEPS, 3, rows, wy, depth), f32),
            vmem((2, rows, size_y, depth), f32),
            vmem((size_y, depth), f32),
            vmem((9, size_y, depth), f32),
            vmem((3, wy, depth), f32),
            vmem((2 * STEPS, depth), f32),
            vmem(observed.shape, f32),
            smem(footprint.shape, jnp.int32),
            smem(owner.shape, jnp.int32),
            vmem(rec_cells.shape, jnp.int32),
            vmem((8, depth), f32),
            vmem((plane, 8, depth), f32),
            vmem((8, depth), f32),
            vmem((8, depth), f32),
            vmem((8, depth), f32),
            vmem((nz, 8, depth), f32),
            vmem((nz, packed, depth), f32),
            vmem((nz, packed, depth), f32),
            vmem((nz, packed, depth), f32),
            vmem((nz, packed, depth), f32),
            dma((8,)),
            dma((4, n_dirs)),
            dma((4, n_dirs)),
            dma((n_dirs,)),
            dma((n_dirs,)),
            dma((plane,)),
            dma((plane,)),
            dma((2,)),
            dma((nz,)),
            dma((nz,)),
            dma((nz,)),
            dma((nz,)),
            dma((nz,)),
            dma((nz,)),
        ],
        compiler_params=pltpu.CompilerParams(
            collective_id=0, has_side_effects=True, vmem_limit_bytes=60 * 1024 * 1024
        ),
    )(cond_h, cond_v, fwd_init, adj_init, observed, footprint, owner, rec_cells)
    return owned, misfit.reshape(())


def solution(mesh):
    placed = (
        P("gx", "gy", None),
        P("gx", "gy", None),
        P("tx", None, "gx", "gy", None),
        P("tx", None, "gx", "gy", None),
        P("tx", None, "gx", "gy", None, None),
        P("tx", "gx", "gy"),
        P("gx", "gy", None),
        P("gx", "gy", None),
    )
    sizes = (mesh.shape["tx"], mesh.shape["gx"], mesh.shape["gy"])
    return jax.shard_map(
        functools.partial(on_device, sizes),
        mesh=mesh,
        in_specs=placed,
        out_specs=(P("gx", "tx", None, None, "gy", None), P()),
        check_vma=False,
    )
```

```python
import functools

import jax
import jax.numpy as jnp
from jax import lax
from jax.experimental import pallas as pl
from jax.experimental.pallas import tpu as pltpu
from jax.sharding import PartitionSpec as P

STEPS = 4
ZREC = 32
STEP_DT = 0.5
HALO = STEPS
LOW = HALO + 1
MESH = pl.DeviceIdType.MESH
DIRS = [(dx, dy) for dx in (-1, 0, 1) for dy in (-1, 0, 1) if (dx, dy) != (0, 0)]


def window_rows(gx_size, size_x):
    return size_x + (HALO if gx_size == 2 else 2 * HALO)


def kernel(
    sizes,
    cond_h, cond_v, fwd, adj, observed_in, footprint_in, owner_in, rec_in,
    out, misfit_out,
    fw, aw, cw, decay, drive, grad, inj_own, inj_in, inj_win, obs_scr,
    observed, footprint, owner, rec_cells,
    mis_own, mis_in, mis_tiles, mis_got, mis_chip, mis_part, give, keep, got, part,
    loc_sem, halo_send, halo_recv, inj_send, inj_recv, mis_send, mis_recv,
    mis_sib_sem, mis_z_send, mis_z_recv,
    sib_send, sib_recv, z_send, z_recv,
):
    n_tx, n_gx, n_gy = sizes
    nz = n_tx // 2
    size_x, size_y, depth = cond_h.shape
    rows_w = window_rows(n_gx, size_x)
    wy = size_y + 2 * HALO
    it, ix, iy = lax.axis_index("tx"), lax.axis_index("gx"), lax.axis_index("gy")
    core = lax.rem(it, 2)
    iz = it // 2
    has = {}
    for dx, dy in DIRS:
        ok = None
        for d, i, n in ((dx, ix, n_gx), (dy, iy, n_gy)):
            if d:
                one = (i > 0) if d < 0 else (i < n - 1)
                ok = one if ok is None else jnp.logical_and(ok, one)
        has[(dx, dy)] = ok
    has_lo, has_hi = has[(-1, 0)], has[(1, 0)]
    start = jnp.where(has_lo, -HALO, 0)

    def plane_partner(k):
        ox, oy = k // n_gy, k % n_gy
        return {"gx": lax.rem(ix + ox, n_gx), "gy": lax.rem(iy + oy, n_gy)}

    sibling = {"tx": it + 1 - 2 * core}

    def z_partner(dz):
        return lax.rem(iz + dz, nz)

    tile_x, tile_y = pl.ds(LOW, size_x), pl.ds(0, size_y)
    locals_ = [
        pltpu.make_async_copy(cond_h, cw.at[0, tile_x, tile_y], loc_sem.at[0]),
        pltpu.make_async_copy(cond_v, cw.at[1, tile_x, tile_y], loc_sem.at[1]),
        pltpu.make_async_copy(fwd.at[0], fw.at[0:6, tile_x, tile_y], loc_sem.at[2]),
        pltpu.make_async_copy(adj.at[0], aw.at[:, tile_x, tile_y], loc_sem.at[3]),
        pltpu.make_async_copy(observed_in, observed, loc_sem.at[4]),
        pltpu.make_async_copy(rec_in, rec_cells, loc_sem.at[5]),
        pltpu.make_async_copy(footprint_in, footprint, loc_sem.at[6]),
        pltpu.make_async_copy(owner_in, owner, loc_sem.at[7]),
    ]
    for c in locals_:
        c.start()

    rows_all = fw.shape[1]
    top = LOW + size_x
    for ref in (cw, fw, aw):
        comps = min(ref.shape[0], 6)
        ref[0:comps, :, size_y:wy] = jnp.zeros((comps, rows_all, wy - size_y, depth), jnp.float32)
        if ref is cw and n_gx == 2:
            continue
        zero_rows = (LOW - 1, top) if n_gx == 2 else (*range(LOW), *range(top, rows_all))
        for r in zero_rows:
            ref[0:comps, r, 0:size_y] = jnp.zeros((comps, size_y, depth), jnp.float32)
    inj_in[...] = jnp.zeros_like(inj_in)

    barrier = pltpu.get_barrier_semaphore()
    for k in range(1, n_gx * n_gy):
        pl.semaphore_signal(barrier, inc=1, device_id=plane_partner(k), device_id_type=MESH)
    pl.semaphore_signal(barrier, inc=1, device_id=sibling, device_id_type=MESH)
    for dz in range(1, nz):
        pl.semaphore_signal(
            barrier, inc=1, device_id={"tx": 2 * z_partner(dz) + core}, device_id_type=MESH
        )
    pl.semaphore_wait(barrier, n_gx * n_gy - 1 + 1 + nz - 1)

    def source(d, size, deep=HALO):
        return pl.ds(0, size) if d == 0 else (pl.ds(size - deep, deep) if d > 0 else pl.ds(0, deep))

    def target_x(d, deep=HALO):
        return tile_x if d == 0 else (pl.ds(LOW - deep, deep) if d > 0 else pl.ds(LOW + size_x, deep))

    def target_y(d):
        return tile_y if d == 0 else (pl.ds(size_y + HALO, HALO) if d > 0 else pl.ds(size_y, HALO))

    def halo_copy(which, d):
        dx, dy = DIRS[d]
        sx, sy = source(dx, size_x), source(dy, size_y)
        tx_, ty_ = target_x(dx), target_y(dy)
        if which < 2:
            sx, tx_ = source(dx, size_x, HALO - 1), target_x(dx, HALO - 1)
        src, dst = {
            0: (cond_h.at[sx, sy], cw.at[0, tx_, ty_]),
            1: (cond_v.at[sx, sy], cw.at[1, tx_, ty_]),
            2: (fwd.at[0, :, sx, sy], fw.at[0:6, tx_, ty_]),
            3: (adj.at[0, :, sx, sy], aw.at[:, tx_, ty_]),
        }[which]
        return pltpu.make_async_remote_copy(
            src_ref=src, dst_ref=dst,
            send_sem=halo_send.at[which, d], recv_sem=halo_recv.at[which, d],
            device_id={"gx": ix + dx, "gy": iy + dy}, device_id_type=MESH,
        )

    def each_dir(fn, conds):
        for d, (dx, dy) in enumerate(DIRS):
            if (dx and n_gx == 1) or (dy and n_gy == 1):
                continue
            pl.when(conds(dx, dy))(functools.partial(fn, d))

    def to_side(dx, dy):
        return has[(dx, dy)]

    def from_side(dx, dy):
        return has[(-dx, -dy)]

    for which in range(3):
        each_dir(lambda d, w=which: halo_copy(w, d).start(), to_side)

    lanes = lax.broadcasted_iota(jnp.int32, (size_y, depth), 1)
    for c in locals_[4:]:
        c.wait()
    highest = lax.Precision.HIGHEST
    rpt = rec_cells.shape[-1]
    cells = rec_cells[0]
    in_y = (lax.broadcasted_iota(jnp.int32, (size_y, rpt), 0) == cells % size_y).astype(jnp.float32)
    in_x = (lax.broadcasted_iota(jnp.int32, (size_x, rpt), 0) == cells // size_y).astype(jnp.float32)
    lane_x = (
        lax.broadcasted_iota(jnp.int32, (size_x, depth), 0)
        == lax.broadcasted_iota(jnp.int32, (size_x, depth), 1) % size_x
    ).astype(jnp.float32)
    lane_k = (
        lax.broadcasted_iota(jnp.int32, (2 * STEPS, depth), 0)
        == lax.broadcasted_iota(jnp.int32, (2 * STEPS, depth), 1) // size_x
    ).astype(jnp.float32)
    for n in range(STEPS):
        obs_scr[2 * n : 2 * n + 2, 0:rpt] = observed[0, n, 0, 0]
    over0 = (((0,), (0,)), ((), ()))
    at_x = lax.dot_general(in_x, lane_x, over0, precision=highest, preferred_element_type=jnp.float32)
    obs_l = at_x * lax.dot_general(
        obs_scr[:, 0:rpt], lane_k, over0, precision=highest, preferred_element_type=jnp.float32
    )
    count = jnp.dot(in_y, at_x, precision=highest, preferred_element_type=jnp.float32)
    obs_sum = jnp.dot(in_y, obs_l, precision=highest, preferred_element_type=jnp.float32)

    for x in sorted({size_x, size_x + HALO, rows_w}):
        fw[6:, LOW + x] = jnp.zeros((3 * STEPS, wy, depth), jnp.float32)
    grad[...] = jnp.zeros_like(grad)

    def wait_in(which):
        locals_[which].wait()
        each_dir(lambda d: halo_copy(which, d).wait_recv(), from_side)

    wait_in(0)
    wait_in(1)
    sub = lax.broadcasted_iota(jnp.int32, (wy, depth), 0)
    lane = lax.broadcasted_iota(jnp.int32, (wy, depth), 1)
    y_hi = jnp.where(has[(0, 1)], 1.0, 0.0)
    y_lo = jnp.where(has[(0, -1)], 1.0, 0.0)
    y_ok = jnp.where(sub < size_y, 1.0, jnp.where(sub < size_y + HALO, y_hi, y_lo))
    half = STEP_DT * y_ok

    chunk = rows_w // 4


    def coefficients(k, carry):
        for i in range(chunk):
            x = start + k * chunk + i
            ok = y_ok * jnp.where(jnp.logical_or(x < size_x, has_hi), 1.0, 0.0)
            for c in range(2):
                rate = 0.25 * cw[c, x + LOW]
                scaled = ok / (1.0 + rate)
                drive[c, x + LOW] = STEP_DT * scaled
                decay[c, x + LOW] = (1.0 - rate) * scaled
        return carry

    lax.fori_loop(0, 4, coefficients, 0)

    def y_next(f):
        return pltpu.roll(f, wy - 1, 0)

    def y_prev(f):
        return pltpu.roll(f, 1, 0)

    def z_next(f):
        return jnp.where(lane == depth - 1, 0.0, pltpu.roll(f, depth - 1, 1))

    def z_prev(f):
        return jnp.where(lane == 0, 0.0, pltpu.roll(f, 1, 1))

    def step_rows(r, load, h, e_dst, after):
        ex, ey, ez = (load(c, r) for c in range(3))
        hp_y, hp_z = h[1, r - 1], h[2, r - 1]
        for i in range(chunk):
            ey_n, ez_n = load(1, r + i + 1), load(2, r + i + 1)
            ex_n = load(0, r + i + 1) if i < chunk - 1 else None
            hx = h[0, r + i] - half * ((y_next(ez) - ez) - (z_next(ey) - ey))
            hy = h[1, r + i] - half * ((z_next(ex) - ex) - (ez_n - ez))
            hz = h[2, r + i] - half * ((ey_n - ey) - (y_next(ex) - ex))
            h[0, r + i] = hx
            h[1, r + i] = hy
            h[2, r + i] = hz
            cx = (hz - y_prev(hz)) - (hy - z_prev(hy))
            cy = (hx - z_prev(hx)) - (hz - hp_z)
            cz = (hy - hp_y) - (hx - y_prev(hx))
            hp_y, hp_z = hy, hz
            dec_h, drv_h = decay[0, r + i], drive[0, r + i]
            dec_v, drv_v = decay[1, r + i], drive[1, r + i]
            new = (dec_h * ex + drv_h * cx, dec_h * ey + drv_h * cy, dec_v * ez + drv_v * cz)
            for c in range(3):
                e_dst[c, r + i] = new[c]
            if after is not None:
                after(r + i, new)
            ex, ey, ez = ex_n, ey_n, ez_n

    def step(load, h, e_dst, after=None):
        def body(k, carry):
            step_rows(start + LOW + k * chunk, load, h, e_dst, after)
            return carry

        lax.fori_loop(0, 4, body, 0)

    wait_in(2)
    each_dir(lambda d: halo_copy(3, d).start(), to_side)
    def forward(n, carry):
        src, dst = jnp.where(n == 0, 0, 3 * n + 3), 3 * n + 6
        step(lambda c, r: fw[src + c, r], fw.at[3:6], fw.at[pl.ds(dst, 3)])
        return carry

    lax.fori_loop(0, STEPS, forward, 0)

    def records(k, rec):
        for x in range(size_x):
            at = k * size_x + x
            e = fw[6 + 3 * (k // 2) + k % 2, LOW + x, 0:size_y]
            rec = jnp.where(lanes == at, pltpu.roll(e, lax.rem(at + depth - ZREC, depth), 1), rec)
        return rec

    rec = lax.fori_loop(0, 2 * STEPS, records, jnp.zeros((size_y, depth), jnp.float32))
    inj_own[...] = count * rec - obs_sum

    def inj_copy(d):
        dx, dy = DIRS[d]
        return pltpu.make_async_remote_copy(
            src_ref=inj_own, dst_ref=inj_in.at[(1 - dx) * 3 + 1 - dy],
            send_sem=inj_send.at[d], recv_sem=inj_recv.at[d],
            device_id={"gx": ix + dx, "gy": iy + dy}, device_id_type=MESH,
        )

    each_dir(lambda d: inj_copy(d).start(), to_side)

    at_rec = lax.dot_general(in_y, rec, over0, precision=highest, preferred_element_type=jnp.float32)
    resid = at_x * at_rec - obs_l
    mis_own[...] = 0.5 * jnp.sum((resid * resid).reshape(rpt // 8, 8, depth), axis=0)

    def mis_copy(k):
        return pltpu.make_async_remote_copy(
            src_ref=mis_own, dst_ref=mis_in.at[k],
            send_sem=mis_send.at[k], recv_sem=mis_recv.at[k],
            device_id=plane_partner(k), device_id_type=MESH,
        )

    for k in range(1, n_gx * n_gy):
        mis_copy(k).start()

    wait_in(3)
    each_dir(lambda d: inj_copy(d).wait_recv(), from_side)
    sub8 = lax.broadcasted_iota(jnp.int32, (2 * HALO, depth), 0)
    for q in range(3):
        own = inj_own[...] if q == 1 else inj_in[q * 3 + 1]
        inj_win[q, 0:size_y] = own
        inj_win[q, size_y:wy] = jnp.where(
            sub8 < HALO,
            inj_in[q * 3 + 2, 0 : 2 * HALO],
            inj_in[q * 3, size_y - 2 * HALO : size_y],
        )

    def mis_sib():
        return pltpu.make_async_remote_copy(
            src_ref=mis_tiles, dst_ref=mis_got,
            send_sem=mis_sib_sem.at[0], recv_sem=mis_sib_sem.at[1],
            device_id=sibling, device_id_type=MESH,
        )

    def mis_z(dz):
        return pltpu.make_async_remote_copy(
            src_ref=mis_chip, dst_ref=mis_part.at[dz],
            send_sem=mis_z_send.at[dz], recv_sem=mis_z_recv.at[dz],
            device_id={"tx": 2 * z_partner(dz) + core}, device_id_type=MESH,
        )

    def misfit_round(n):
        @pl.when(n == STEPS - 1)
        def _():
            total = mis_own[...]
            for k in range(1, n_gx * n_gy):
                mis_copy(k).wait_recv()
                total = total + mis_in[k]
            mis_tiles[...] = total
            mis_sib().start()

        @pl.when(n == STEPS - 2)
        def _():
            mis_sib().wait_recv()
            mis_chip[...] = mis_tiles[...] + mis_got[...]
            for dz in range(1, nz):
                mis_z(dz).start()

        @pl.when(n == STEPS - 3)
        def _():
            total = mis_chip[...]
            for dz in range(1, nz):
                mis_z(dz).wait_recv()
                total = total + mis_part[dz]
            misfit_out[0, 0] = jnp.sum(total)

    def adjoint(back, carry):
        n = STEPS - 1 - back

        def load(c, r):
            e = aw[c, r]
            if c == 2:
                return e
            x = r - LOW + size_x
            at = (2 * n + c) * size_x + lax.rem(x, size_x)
            moved = pltpu.roll(inj_win[x // size_x], lax.rem(ZREC + depth - at, depth), 1)
            return e + jnp.where(lane == ZREC, moved, 0.0)

        def add_gradient(r, new):
            stored = [fw[6 + 3 * n + c, r, 0:size_y] for c in range(3)]
            mine = [f[0:size_y] for f in new]
            grad[0, r] = grad[0, r] + mine[0] * stored[0] + mine[1] * stored[1]
            grad[1, r] = grad[1, r] + mine[2] * stored[2]

        step(load, aw.at[3:6], aw.at[0:3], add_gradient)
        misfit_round(n)
        return carry

    lax.fori_loop(0, STEPS, adjoint, 0)

    flag = footprint[0, 0, 0].astype(jnp.float32)
    block = size_x // n_tx

    def ordered(dst, dz, to_core):
        z = z_partner(dz)
        first = owner[0, 0, 2 * z + to_core] * block
        for c in range(2):
            for b in range(block):
                at = (c * block + b) * size_y
                dst[dz, at : at + size_y] = flag * grad[c, LOW + first + b]

    def sib_copy(dz):
        return pltpu.make_async_remote_copy(
            src_ref=give.at[dz], dst_ref=got.at[dz],
            send_sem=sib_send.at[dz], recv_sem=sib_recv.at[dz],
            device_id=sibling, device_id_type=MESH,
        )

    def z_copy(dz):
        return pltpu.make_async_remote_copy(
            src_ref=keep.at[dz], dst_ref=part.at[dz],
            send_sem=z_send.at[dz], recv_sem=z_recv.at[dz],
            device_id={"tx": 2 * z_partner(dz) + core}, device_id_type=MESH,
        )

    order = list(range(1, nz)) + [0]
    for dz in order:
        ordered(give, dz, 1 - core)
        sib_copy(dz).start()
    for dz in order:
        ordered(keep, dz, core)
    for dz in order:
        sib_copy(dz).wait_recv()
        keep[dz] = keep[dz] + got[dz]
        if dz:
            z_copy(dz).start()
    for dz in range(1, nz):
        z_copy(dz).wait_recv()
    total = keep[0]
    for dz in range(1, nz):
        total = total + part[dz]
    for c in range(2):
        for b in range(block):
            at = (c * block + b) * size_y
            out[0, 0, c, b] = total[at : at + size_y]

    for which in range(4):
        each_dir(lambda d, w=which: halo_copy(w, d).wait_send(), to_side)
    each_dir(lambda d: inj_copy(d).wait_send(), to_side)
    for k in range(1, n_gx * n_gy):
        mis_copy(k).wait_send()
    mis_sib().wait_send()
    for dz in range(1, nz):
        mis_z(dz).wait_send()
    for dz in order:
        sib_copy(dz).wait_send()
    for dz in range(1, nz):
        z_copy(dz).wait_send()


def on_device(sizes, cond_h, cond_v, fwd_init, adj_init, observed, footprint, owner, rec_cells):
    n_tx, n_gx, n_gy = sizes
    nz = n_tx // 2
    size_x, size_y, depth = cond_h.shape
    rows_w = window_rows(n_gx, size_x)
    rows = LOW + rows_w + 1
    wy = size_y + 2 * HALO
    block = size_x // n_tx
    packed = 2 * block * size_y
    f32 = jnp.float32
    n_dirs = len(DIRS)
    plane = n_gx * n_gy
    dma = pltpu.SemaphoreType.DMA
    hbm, vmem, smem = pl.ANY, pltpu.VMEM, pltpu.SMEM
    owned, misfit = pl.pallas_call(
        functools.partial(kernel, sizes),
        out_shape=(
            jax.ShapeDtypeStruct((1, 1, 2, block, size_y, depth), f32),
            jax.ShapeDtypeStruct((1, 1), f32),
        ),
        in_specs=[
            pl.BlockSpec(memory_space=s) for s in [hbm] * 8
        ],
        out_specs=(pl.BlockSpec(memory_space=vmem), pl.BlockSpec(memory_space=smem)),
        scratch_shapes=[
            vmem((6 + 3 * STEPS, rows, wy, depth), f32),
            vmem((6, rows, wy, depth), f32),
            vmem((2, rows, wy, depth), f32),
            vmem((2, rows, wy, depth), f32),
            vmem((2, rows, wy, depth), f32),
            vmem((2, rows, size_y, depth), f32),
            vmem((size_y, depth), f32),
            vmem((9, size_y, depth), f32),
            vmem((3, wy, depth), f32),
            vmem((2 * STEPS, depth), f32),
            vmem(observed.shape, f32),
            smem(footprint.shape, jnp.int32),
            smem(owner.shape, jnp.int32),
            vmem(rec_cells.shape, jnp.int32),
            vmem((8, depth), f32),
            vmem((plane, 8, depth), f32),
            vmem((8, depth), f32),
            vmem((8, depth), f32),
            vmem((8, depth), f32),
            vmem((nz, 8, depth), f32),
            vmem((nz, packed, depth), f32),
            vmem((nz, packed, depth), f32),
            vmem((nz, packed, depth), f32),
            vmem((nz, packed, depth), f32),
            dma((8,)),
            dma((4, n_dirs)),
            dma((4, n_dirs)),
            dma((n_dirs,)),
            dma((n_dirs,)),
            dma((plane,)),
            dma((plane,)),
            dma((2,)),
            dma((nz,)),
            dma((nz,)),
            dma((nz,)),
            dma((nz,)),
            dma((nz,)),
            dma((nz,)),
        ],
        compiler_params=pltpu.CompilerParams(
            collective_id=0, has_side_effects=True, vmem_limit_bytes=60 * 1024 * 1024
        ),
    )(cond_h, cond_v, fwd_init, adj_init, observed, footprint, owner, rec_cells)
    return owned, misfit.reshape(())


def solution(mesh):
    placed = (
        P("gx", "gy", None),
        P("gx", "gy", None),
        P("tx", None, "gx", "gy", None),
        P("tx", None, "gx", "gy", None),
        P("tx", None, "gx", "gy", None, None),
        P("tx", "gx", "gy"),
        P("gx", "gy", None),
        P("gx", "gy", None),
    )
    sizes = (mesh.shape["tx"], mesh.shape["gx"], mesh.shape["gy"])
    return jax.shard_map(
        functools.partial(on_device, sizes),
        mesh=mesh,
        in_specs=placed,
        out_specs=(P("gx", "tx", None, None, "gy", None), P()),
        check_vma=False,
    )
```

```python
import functools

import jax
import jax.numpy as jnp
from jax import lax
from jax.experimental import pallas as pl
from jax.experimental.pallas import tpu as pltpu
from jax.sharding import PartitionSpec as P

STEPS = 4
ZREC = 32
STEP_DT = 0.5
HALO = STEPS
LOW = HALO + 1
MESH = pl.DeviceIdType.MESH
DIRS = [(dx, dy) for dx in (-1, 0, 1) for dy in (-1, 0, 1) if (dx, dy) != (0, 0)]


def window_rows(gx_size, size_x):
    return size_x + (HALO if gx_size == 2 else 2 * HALO)


def kernel(
    sizes,
    cond_h, cond_v, fwd, adj, observed_in, footprint_in, owner_in, rec_in,
    out, misfit_out,
    fw, aw, cw, decay, drive, kept, grad, inj_own, inj_in, inj_win, obs_scr,
    observed, footprint, owner, rec_cells,
    mis_own, mis_in, give, keep, got, part,
    loc_sem, halo_send, halo_recv, inj_send, inj_recv, mis_send, mis_recv,
    sib_send, sib_recv, z_send, z_recv,
):
    n_tx, n_gx, n_gy = sizes
    nz = n_tx // 2
    size_x, size_y, depth = cond_h.shape
    rows_w = window_rows(n_gx, size_x)
    wy = size_y + 2 * HALO
    it, ix, iy = lax.axis_index("tx"), lax.axis_index("gx"), lax.axis_index("gy")
    core = lax.rem(it, 2)
    iz = it // 2
    has = {}
    for dx, dy in DIRS:
        ok = None
        for d, i, n in ((dx, ix, n_gx), (dy, iy, n_gy)):
            if d:
                one = (i > 0) if d < 0 else (i < n - 1)
                ok = one if ok is None else jnp.logical_and(ok, one)
        has[(dx, dy)] = ok
    has_lo, has_hi = has[(-1, 0)], has[(1, 0)]
    start = jnp.where(has_lo, -HALO, 0)

    def plane_partner(k):
        ox, oy = k // n_gy, k % n_gy
        return {"gx": lax.rem(ix + ox, n_gx), "gy": lax.rem(iy + oy, n_gy)}

    sibling = {"tx": it + 1 - 2 * core}

    def z_partner(dz):
        return lax.rem(iz + dz, nz)

    tile_x, tile_y = pl.ds(LOW, size_x), pl.ds(0, size_y)
    locals_ = [
        pltpu.make_async_copy(cond_h, cw.at[0, tile_x, tile_y], loc_sem.at[0]),
        pltpu.make_async_copy(cond_v, cw.at[1, tile_x, tile_y], loc_sem.at[1]),
        pltpu.make_async_copy(fwd.at[0], fw.at[:, tile_x, tile_y], loc_sem.at[2]),
        pltpu.make_async_copy(adj.at[0], aw.at[:, tile_x, tile_y], loc_sem.at[3]),
        pltpu.make_async_copy(observed_in, observed, loc_sem.at[4]),
        pltpu.make_async_copy(rec_in, rec_cells, loc_sem.at[5]),
        pltpu.make_async_copy(footprint_in, footprint, loc_sem.at[6]),
        pltpu.make_async_copy(owner_in, owner, loc_sem.at[7]),
    ]
    for c in locals_:
        c.start()

    rows_all = fw.shape[1]
    top = LOW + size_x
    for ref in (cw, fw, aw):
        comps = ref.shape[0]
        ref[:, :, size_y:wy] = jnp.zeros((comps, rows_all, wy - size_y, depth), jnp.float32)
        if ref is cw and n_gx == 2:
            continue
        zero_rows = (LOW - 1, top) if n_gx == 2 else (*range(LOW), *range(top, rows_all))
        for r in zero_rows:
            ref[:, r, 0:size_y] = jnp.zeros((comps, size_y, depth), jnp.float32)
    inj_in[...] = jnp.zeros_like(inj_in)

    barrier = pltpu.get_barrier_semaphore()
    for k in range(1, n_gx * n_gy):
        pl.semaphore_signal(barrier, inc=1, device_id=plane_partner(k), device_id_type=MESH)
    pl.semaphore_signal(barrier, inc=1, device_id=sibling, device_id_type=MESH)
    for dz in range(1, nz):
        pl.semaphore_signal(
            barrier, inc=1, device_id={"tx": 2 * z_partner(dz) + core}, device_id_type=MESH
        )
    pl.semaphore_wait(barrier, n_gx * n_gy - 1 + 1 + nz - 1)

    def source(d, size, deep=HALO):
        return pl.ds(0, size) if d == 0 else (pl.ds(size - deep, deep) if d > 0 else pl.ds(0, deep))

    def target_x(d, deep=HALO):
        return tile_x if d == 0 else (pl.ds(LOW - deep, deep) if d > 0 else pl.ds(LOW + size_x, deep))

    def target_y(d):
        return tile_y if d == 0 else (pl.ds(size_y + HALO, HALO) if d > 0 else pl.ds(size_y, HALO))

    def halo_copy(which, d):
        dx, dy = DIRS[d]
        sx, sy = source(dx, size_x), source(dy, size_y)
        tx_, ty_ = target_x(dx), target_y(dy)
        if which < 2:
            sx, tx_ = source(dx, size_x, HALO - 1), target_x(dx, HALO - 1)
        src, dst = {
            0: (cond_h.at[sx, sy], cw.at[0, tx_, ty_]),
            1: (cond_v.at[sx, sy], cw.at[1, tx_, ty_]),
            2: (fwd.at[0, :, sx, sy], fw.at[:, tx_, ty_]),
            3: (adj.at[0, :, sx, sy], aw.at[:, tx_, ty_]),
        }[which]
        return pltpu.make_async_remote_copy(
            src_ref=src, dst_ref=dst,
            send_sem=halo_send.at[which, d], recv_sem=halo_recv.at[which, d],
            device_id={"gx": ix + dx, "gy": iy + dy}, device_id_type=MESH,
        )

    def each_dir(fn, conds):
        for d, (dx, dy) in enumerate(DIRS):
            if (dx and n_gx == 1) or (dy and n_gy == 1):
                continue
            pl.when(conds(dx, dy))(functools.partial(fn, d))

    def to_side(dx, dy):
        return has[(dx, dy)]

    def from_side(dx, dy):
        return has[(-dx, -dy)]

    for which in range(3):
        each_dir(lambda d, w=which: halo_copy(w, d).start(), to_side)

    lanes = lax.broadcasted_iota(jnp.int32, (size_y, depth), 1)
    for c in locals_[4:]:
        c.wait()
    highest = lax.Precision.HIGHEST
    rpt = rec_cells.shape[-1]
    cells = rec_cells[0]
    in_y = (lax.broadcasted_iota(jnp.int32, (size_y, rpt), 0) == cells % size_y).astype(jnp.float32)
    in_x = (lax.broadcasted_iota(jnp.int32, (size_x, rpt), 0) == cells // size_y).astype(jnp.float32)
    lane_x = (
        lax.broadcasted_iota(jnp.int32, (size_x, depth), 0)
        == lax.broadcasted_iota(jnp.int32, (size_x, depth), 1) % size_x
    ).astype(jnp.float32)
    lane_k = (
        lax.broadcasted_iota(jnp.int32, (2 * STEPS, depth), 0)
        == lax.broadcasted_iota(jnp.int32, (2 * STEPS, depth), 1) // size_x
    ).astype(jnp.float32)
    for n in range(STEPS):
        obs_scr[2 * n : 2 * n + 2, 0:rpt] = observed[0, n, 0, 0]
    over0 = (((0,), (0,)), ((), ()))
    at_x = lax.dot_general(in_x, lane_x, over0, precision=highest, preferred_element_type=jnp.float32)
    obs_l = at_x * lax.dot_general(
        obs_scr[:, 0:rpt], lane_k, over0, precision=highest, preferred_element_type=jnp.float32
    )
    count = jnp.dot(in_y, at_x, precision=highest, preferred_element_type=jnp.float32)
    obs_sum = jnp.dot(in_y, obs_l, precision=highest, preferred_element_type=jnp.float32)

    for n in range(STEPS):
        for x in sorted({size_x, size_x + HALO, rows_w}):
            kept[n, :, LOW + x] = jnp.zeros((3, wy, depth), jnp.float32)

    def wait_in(which):
        locals_[which].wait()
        each_dir(lambda d: halo_copy(which, d).wait_recv(), from_side)

    wait_in(0)
    wait_in(1)
    sub = lax.broadcasted_iota(jnp.int32, (wy, depth), 0)
    lane = lax.broadcasted_iota(jnp.int32, (wy, depth), 1)
    y_hi = jnp.where(has[(0, 1)], 1.0, 0.0)
    y_lo = jnp.where(has[(0, -1)], 1.0, 0.0)
    y_ok = jnp.where(sub < size_y, 1.0, jnp.where(sub < size_y + HALO, y_hi, y_lo))
    half = STEP_DT * y_ok

    def span(j):
        if n_gx == 2:
            gone = j - j % 2
            return jnp.where(has_lo, gone - HALO, 0), (rows_w - gone) // 2, 2
        return start, 8, rows_w // 8


    def coefficients(k, carry):
        for i in range(rows_w // 4):
            x = start + k * (rows_w // 4) + i
            ok = y_ok * jnp.where(jnp.logical_or(x < size_x, has_hi), 1.0, 0.0)
            for c in range(2):
                rate = 0.25 * cw[c, x + LOW]
                scaled = ok / (1.0 + rate)
                drive[c, x + LOW] = STEP_DT * scaled
                decay[c, x + LOW] = (1.0 - rate) * scaled
        return carry

    lax.fori_loop(0, 4, coefficients, 0)

    def y_next(f):
        return pltpu.roll(f, wy - 1, 0)

    def y_prev(f):
        return pltpu.roll(f, 1, 0)

    def z_next(f):
        return jnp.where(lane == depth - 1, 0.0, pltpu.roll(f, depth - 1, 1))

    def z_prev(f):
        return jnp.where(lane == 0, 0.0, pltpu.roll(f, 1, 1))

    def step_rows(r, chunk, e_src, h, e_dst, after):
        ex, ey, ez = (e_src[c, r] for c in range(3))
        hp_y, hp_z = h[1, r - 1], h[2, r - 1]
        for i in range(chunk):
            ey_n, ez_n = e_src[1, r + i + 1], e_src[2, r + i + 1]
            ex_n = e_src[0, r + i + 1] if i < chunk - 1 else None
            hx = h[0, r + i] - half * ((y_next(ez) - ez) - (z_next(ey) - ey))
            hy = h[1, r + i] - half * ((z_next(ex) - ex) - (ez_n - ez))
            hz = h[2, r + i] - half * ((ey_n - ey) - (y_next(ex) - ex))
            h[0, r + i] = hx
            h[1, r + i] = hy
            h[2, r + i] = hz
            cx = (hz - y_prev(hz)) - (hy - z_prev(hy))
            cy = (hx - z_prev(hx)) - (hz - hp_z)
            cz = (hy - hp_y) - (hx - y_prev(hx))
            hp_y, hp_z = hy, hz
            dec_h, drv_h = decay[0, r + i], drive[0, r + i]
            dec_v, drv_v = decay[1, r + i], drive[1, r + i]
            new = (dec_h * ex + drv_h * cx, dec_h * ey + drv_h * cy, dec_v * ez + drv_v * cz)
            for c in range(3):
                e_dst[c, r + i] = new[c]
            if after is not None:
                after(r + i, new)
            ex, ey, ez = ex_n, ey_n, ez_n

    def step(j, e_src, h, e_dst, after=None):
        first, chunk, chunks = span(j)

        def body(k, carry):
            step_rows(first + LOW + k * chunk, chunk, e_src, h, e_dst, after)
            return carry

        lax.fori_loop(0, chunks, body, 0)

    each_dir(lambda d: halo_copy(3, d).start(), to_side)
    wait_in(2)
    for n in range(STEPS):
        step(n, fw.at[0:3] if n == 0 else kept.at[n - 1], fw.at[3:6], kept.at[n])

    rec = jnp.zeros((size_y, depth), jnp.float32)
    for n in range(STEPS):
        for c in range(2):
            for x in range(size_x):
                at = (2 * n + c) * size_x + x
                e = kept[n, c, LOW + x, 0:size_y]
                rec = jnp.where(lanes == at, pltpu.roll(e, (at - ZREC) % depth, 1), rec)
    inj_own[...] = count * rec - obs_sum

    def inj_copy(d):
        dx, dy = DIRS[d]
        return pltpu.make_async_remote_copy(
            src_ref=inj_own, dst_ref=inj_in.at[(1 - dx) * 3 + 1 - dy],
            send_sem=inj_send.at[d], recv_sem=inj_recv.at[d],
            device_id={"gx": ix + dx, "gy": iy + dy}, device_id_type=MESH,
        )

    each_dir(lambda d: inj_copy(d).start(), to_side)

    at_rec = lax.dot_general(in_y, rec, over0, precision=highest, preferred_element_type=jnp.float32)
    resid = at_x * at_rec - obs_l
    mis_own[...] = 0.5 * jnp.sum((resid * resid).reshape(rpt // 8, 8, depth), axis=0)

    def mis_copy(k):
        return pltpu.make_async_remote_copy(
            src_ref=mis_own, dst_ref=mis_in.at[k],
            send_sem=mis_send.at[k], recv_sem=mis_recv.at[k],
            device_id=plane_partner(k), device_id_type=MESH,
        )

    for k in range(1, n_gx * n_gy):
        mis_copy(k).start()

    wait_in(3)
    each_dir(lambda d: inj_copy(d).wait_recv(), from_side)
    sub8 = lax.broadcasted_iota(jnp.int32, (2 * HALO, depth), 0)
    for q in range(3):
        own = inj_own[...] if q == 1 else inj_in[q * 3 + 1]
        inj_win[q, 0:size_y] = own
        inj_win[q, size_y:wy] = jnp.where(
            sub8 < HALO,
            inj_in[q * 3 + 2, 0 : 2 * HALO],
            inj_in[q * 3, size_y - 2 * HALO : size_y],
        )

    for n in reversed(range(STEPS)):
        first, chunk, chunks = span(STEPS - 1 - n)

        def inject(k, carry, n=n, first=first, chunk=chunk):
            for i in range(chunk):
                x = first + k * chunk + i
                plane = inj_win[(x + size_x) // size_x]
                for c in range(2):
                    at = (2 * n + c) * size_x + lax.rem(x + size_x, size_x)
                    moved = pltpu.roll(plane, lax.rem(ZREC + depth - at, depth), 1)
                    aw[c, x + LOW] = aw[c, x + LOW] + jnp.where(lane == ZREC, moved, 0.0)
            return carry

        lax.fori_loop(0, chunks, inject, 0)

        def add_gradient(r, new, n=n):
            tile = slice(0, size_y)
            g_h = new[0][tile] * kept[n, 0, r, tile] + new[1][tile] * kept[n, 1, r, tile]
            g_v = new[2][tile] * kept[n, 2, r, tile]
            if n < STEPS - 1:
                g_h = grad[0, r] + g_h
                g_v = grad[1, r] + g_v
            grad[0, r] = g_h
            grad[1, r] = g_v

        step(STEPS - 1 - n, aw.at[0:3], aw.at[3:6], aw.at[0:3], add_gradient)

    for k in range(1, n_gx * n_gy):
        mis_copy(k).wait_recv()
    misfit = mis_own[...]
    for k in range(1, n_gx * n_gy):
        misfit = misfit + mis_in[k]

    flag = footprint[0, 0, 0].astype(jnp.float32)
    block = size_x // n_tx
    cells_rows = 2 * block * size_y

    def ordered(dst, dz, to_core):
        z = z_partner(dz)
        first = owner[0, 0, 2 * z + to_core] * block
        for c in range(2):
            for b in range(block):
                at = (c * block + b) * size_y
                dst[dz, at : at + size_y] = flag * grad[c, LOW + first + b]
        dst[dz, cells_rows : cells_rows + 8] = misfit

    def sib_copy(dz):
        return pltpu.make_async_remote_copy(
            src_ref=give.at[dz], dst_ref=got.at[dz],
            send_sem=sib_send.at[dz], recv_sem=sib_recv.at[dz],
            device_id=sibling, device_id_type=MESH,
        )

    def z_copy(dz):
        return pltpu.make_async_remote_copy(
            src_ref=keep.at[dz], dst_ref=part.at[dz],
            send_sem=z_send.at[dz], recv_sem=z_recv.at[dz],
            device_id={"tx": 2 * z_partner(dz) + core}, device_id_type=MESH,
        )

    order = list(range(1, nz)) + [0]
    for dz in order:
        ordered(give, dz, 1 - core)
        sib_copy(dz).start()
    for dz in order:
        ordered(keep, dz, core)
    for dz in order:
        sib_copy(dz).wait_recv()
        keep[dz] = keep[dz] + got[dz]
        if dz:
            z_copy(dz).start()
    for dz in range(1, nz):
        z_copy(dz).wait_recv()
    total = keep[0]
    for dz in range(1, nz):
        total = total + part[dz]
    for c in range(2):
        for b in range(block):
            at = (c * block + b) * size_y
            out[0, 0, c, b] = total[at : at + size_y]
    misfit_out[0, 0] = jnp.sum(total[cells_rows : cells_rows + 8])

    for which in range(4):
        each_dir(lambda d, w=which: halo_copy(w, d).wait_send(), to_side)
    each_dir(lambda d: inj_copy(d).wait_send(), to_side)
    for k in range(1, n_gx * n_gy):
        mis_copy(k).wait_send()
    for dz in order:
        sib_copy(dz).wait_send()
    for dz in range(1, nz):
        z_copy(dz).wait_send()


def on_device(sizes, cond_h, cond_v, fwd_init, adj_init, observed, footprint, owner, rec_cells):
    n_tx, n_gx, n_gy = sizes
    nz = n_tx // 2
    size_x, size_y, depth = cond_h.shape
    rows_w = window_rows(n_gx, size_x)
    rows = LOW + rows_w + 1
    wy = size_y + 2 * HALO
    block = size_x // n_tx
    packed = 2 * block * size_y + 8
    f32 = jnp.float32
    n_dirs = len(DIRS)
    plane = n_gx * n_gy
    dma = pltpu.SemaphoreType.DMA
    hbm, vmem, smem = pl.ANY, pltpu.VMEM, pltpu.SMEM
    owned, misfit = pl.pallas_call(
        functools.partial(kernel, sizes),
        out_shape=(
            jax.ShapeDtypeStruct((1, 1, 2, block, size_y, depth), f32),
            jax.ShapeDtypeStruct((1, 1), f32),
        ),
        in_specs=[
            pl.BlockSpec(memory_space=s) for s in [hbm] * 8
        ],
        out_specs=(pl.BlockSpec(memory_space=vmem), pl.BlockSpec(memory_space=smem)),
        scratch_shapes=[
            vmem((6, rows, wy, depth), f32),
            vmem((6, rows, wy, depth), f32),
            vmem((2, rows, wy, depth), f32),
            vmem((2, rows, wy, depth), f32),
            vmem((2, rows, wy, depth), f32),
            vmem((STEPS, 3, rows, wy, depth), f32),
            vmem((2, rows, size_y, depth), f32),
            vmem((size_y, depth), f32),
            vmem((9, size_y, depth), f32),
            vmem((3, wy, depth), f32),
            vmem((2 * STEPS, depth), f32),
            vmem(observed.shape, f32),
            smem(footprint.shape, jnp.int32),
            smem(owner.shape, jnp.int32),
            vmem(rec_cells.shape, jnp.int32),
            vmem((8, depth), f32),
            vmem((plane, 8, depth), f32),
            vmem((nz, packed, depth), f32),
            vmem((nz, packed, depth), f32),
            vmem((nz, packed, depth), f32),
            vmem((nz, packed, depth), f32),
            dma((8,)),
            dma((4, n_dirs)),
            dma((4, n_dirs)),
            dma((n_dirs,)),
            dma((n_dirs,)),
            dma((plane,)),
            dma((plane,)),
            dma((nz,)),
            dma((nz,)),
            dma((nz,)),
            dma((nz,)),
        ],
        compiler_params=pltpu.CompilerParams(
            collective_id=0, has_side_effects=True, vmem_limit_bytes=60 * 1024 * 1024
        ),
    )(cond_h, cond_v, fwd_init, adj_init, observed, footprint, owner, rec_cells)
    return owned, misfit.reshape(())


def solution(mesh):
    placed = (
        P("gx", "gy", None),
        P("gx", "gy", None),
        P("tx", None, "gx", "gy", None),
        P("tx", None, "gx", "gy", None),
        P("tx", None, "gx", "gy", None, None),
        P("tx", "gx", "gy"),
        P("gx", "gy", None),
        P("gx", "gy", None),
    )
    sizes = (mesh.shape["tx"], mesh.shape["gx"], mesh.shape["gy"])
    return jax.shard_map(
        functools.partial(on_device, sizes),
        mesh=mesh,
        in_specs=placed,
        out_specs=(P("gx", "tx", None, None, "gy", None), P()),
        check_vma=False,
    )
```

```python
import functools

import jax
import jax.numpy as jnp
from jax import lax
from jax.experimental import pallas as pl
from jax.experimental.pallas import tpu as pltpu
from jax.sharding import PartitionSpec as P

STEPS = 4
ZREC = 32
STEP_DT = 0.5
HALO = STEPS
LOW = HALO + 1
MESH = pl.DeviceIdType.MESH
DIRS = [(dx, dy) for dx in (-1, 0, 1) for dy in (-1, 0, 1) if (dx, dy) != (0, 0)]


def window_rows(gx_size, size_x):
    return size_x + (HALO if gx_size == 2 else 2 * HALO)


def kernel(
    sizes,
    cond_h, cond_v, fwd, adj, observed_in, footprint_in, owner_in, rec_in,
    out, misfit_out,
    fw, aw, cw, decay, drive, kept, grad, inj_own, inj_in, inj_win, obs_scr,
    observed, footprint, owner, rec_cells,
    mis_own, mis_in, give, keep, got, part,
    loc_sem, halo_send, halo_recv, inj_send, inj_recv, mis_send, mis_recv,
    sib_send, sib_recv, z_send, z_recv,
):
    n_tx, n_gx, n_gy = sizes
    nz = n_tx // 2
    size_x, size_y, depth = cond_h.shape
    rows_w = window_rows(n_gx, size_x)
    wy = size_y + 2 * HALO
    it, ix, iy = lax.axis_index("tx"), lax.axis_index("gx"), lax.axis_index("gy")
    core = lax.rem(it, 2)
    iz = it // 2
    has = {}
    for dx, dy in DIRS:
        ok = None
        for d, i, n in ((dx, ix, n_gx), (dy, iy, n_gy)):
            if d:
                one = (i > 0) if d < 0 else (i < n - 1)
                ok = one if ok is None else jnp.logical_and(ok, one)
        has[(dx, dy)] = ok
    has_lo, has_hi = has[(-1, 0)], has[(1, 0)]
    start = jnp.where(has_lo, -HALO, 0)

    def plane_partner(k):
        ox, oy = k // n_gy, k % n_gy
        return {"gx": lax.rem(ix + ox, n_gx), "gy": lax.rem(iy + oy, n_gy)}

    sibling = {"tx": it + 1 - 2 * core}

    def z_partner(dz):
        return lax.rem(iz + dz, nz)

    tile_x, tile_y = pl.ds(LOW, size_x), pl.ds(0, size_y)
    locals_ = [
        pltpu.make_async_copy(cond_h, cw.at[0, tile_x, tile_y], loc_sem.at[0]),
        pltpu.make_async_copy(cond_v, cw.at[1, tile_x, tile_y], loc_sem.at[1]),
        pltpu.make_async_copy(fwd.at[0], fw.at[:, tile_x, tile_y], loc_sem.at[2]),
        pltpu.make_async_copy(adj.at[0], aw.at[:, tile_x, tile_y], loc_sem.at[3]),
        pltpu.make_async_copy(observed_in, observed, loc_sem.at[4]),
        pltpu.make_async_copy(rec_in, rec_cells, loc_sem.at[5]),
        pltpu.make_async_copy(footprint_in, footprint, loc_sem.at[6]),
        pltpu.make_async_copy(owner_in, owner, loc_sem.at[7]),
    ]
    for c in locals_:
        c.start()

    rows_all = fw.shape[1]
    top = LOW + size_x
    for ref in (cw, fw, aw):
        comps = ref.shape[0]
        ref[:, :, size_y:wy] = jnp.zeros((comps, rows_all, wy - size_y, depth), jnp.float32)
        if ref is cw and n_gx == 2:
            continue
        zero_rows = (LOW - 1, top) if n_gx == 2 else (*range(LOW), *range(top, rows_all))
        for r in zero_rows:
            ref[:, r, 0:size_y] = jnp.zeros((comps, size_y, depth), jnp.float32)
    inj_in[...] = jnp.zeros_like(inj_in)

    barrier = pltpu.get_barrier_semaphore()
    for k in range(1, n_gx * n_gy):
        pl.semaphore_signal(barrier, inc=1, device_id=plane_partner(k), device_id_type=MESH)
    pl.semaphore_signal(barrier, inc=1, device_id=sibling, device_id_type=MESH)
    for dz in range(1, nz):
        pl.semaphore_signal(
            barrier, inc=1, device_id={"tx": 2 * z_partner(dz) + core}, device_id_type=MESH
        )
    pl.semaphore_wait(barrier, n_gx * n_gy - 1 + 1 + nz - 1)

    def source(d, size, deep=HALO):
        return pl.ds(0, size) if d == 0 else (pl.ds(size - deep, deep) if d > 0 else pl.ds(0, deep))

    def target_x(d, deep=HALO):
        return tile_x if d == 0 else (pl.ds(LOW - deep, deep) if d > 0 else pl.ds(LOW + size_x, deep))

    def target_y(d):
        return tile_y if d == 0 else (pl.ds(size_y + HALO, HALO) if d > 0 else pl.ds(size_y, HALO))

    def halo_copy(which, d):
        dx, dy = DIRS[d]
        sx, sy = source(dx, size_x), source(dy, size_y)
        tx_, ty_ = target_x(dx), target_y(dy)
        if which < 2:
            sx, tx_ = source(dx, size_x, HALO - 1), target_x(dx, HALO - 1)
        src, dst = {
            0: (cond_h.at[sx, sy], cw.at[0, tx_, ty_]),
            1: (cond_v.at[sx, sy], cw.at[1, tx_, ty_]),
            2: (fwd.at[0, :, sx, sy], fw.at[:, tx_, ty_]),
            3: (adj.at[0, :, sx, sy], aw.at[:, tx_, ty_]),
        }[which]
        return pltpu.make_async_remote_copy(
            src_ref=src, dst_ref=dst,
            send_sem=halo_send.at[which, d], recv_sem=halo_recv.at[which, d],
            device_id={"gx": ix + dx, "gy": iy + dy}, device_id_type=MESH,
        )

    def each_dir(fn, conds):
        for d, (dx, dy) in enumerate(DIRS):
            if (dx and n_gx == 1) or (dy and n_gy == 1):
                continue
            pl.when(conds(dx, dy))(functools.partial(fn, d))

    def to_side(dx, dy):
        return has[(dx, dy)]

    def from_side(dx, dy):
        return has[(-dx, -dy)]

    for which in range(3):
        each_dir(lambda d, w=which: halo_copy(w, d).start(), to_side)

    lanes = lax.broadcasted_iota(jnp.int32, (size_y, depth), 1)
    for c in locals_[4:]:
        c.wait()
    highest = lax.Precision.HIGHEST
    rpt = rec_cells.shape[-1]
    cells = rec_cells[0]
    in_y = (lax.broadcasted_iota(jnp.int32, (size_y, rpt), 0) == cells % size_y).astype(jnp.float32)
    in_x = (lax.broadcasted_iota(jnp.int32, (size_x, rpt), 0) == cells // size_y).astype(jnp.float32)
    lane_x = (
        lax.broadcasted_iota(jnp.int32, (size_x, depth), 0)
        == lax.broadcasted_iota(jnp.int32, (size_x, depth), 1) % size_x
    ).astype(jnp.float32)
    lane_k = (
        lax.broadcasted_iota(jnp.int32, (2 * STEPS, depth), 0)
        == lax.broadcasted_iota(jnp.int32, (2 * STEPS, depth), 1) // size_x
    ).astype(jnp.float32)
    for n in range(STEPS):
        obs_scr[2 * n : 2 * n + 2, 0:rpt] = observed[0, n, 0, 0]
    over0 = (((0,), (0,)), ((), ()))
    at_x = lax.dot_general(in_x, lane_x, over0, precision=highest, preferred_element_type=jnp.float32)
    obs_l = at_x * lax.dot_general(
        obs_scr[:, 0:rpt], lane_k, over0, precision=highest, preferred_element_type=jnp.float32
    )
    count = jnp.dot(in_y, at_x, precision=highest, preferred_element_type=jnp.float32)
    obs_sum = jnp.dot(in_y, obs_l, precision=highest, preferred_element_type=jnp.float32)

    for n in range(STEPS):
        for x in sorted({size_x, size_x + HALO, rows_w}):
            kept[n, :, LOW + x] = jnp.zeros((3, wy, depth), jnp.float32)

    def wait_in(which):
        locals_[which].wait()
        each_dir(lambda d: halo_copy(which, d).wait_recv(), from_side)

    wait_in(0)
    wait_in(1)
    sub = lax.broadcasted_iota(jnp.int32, (wy, depth), 0)
    lane = lax.broadcasted_iota(jnp.int32, (wy, depth), 1)
    y_hi = jnp.where(has[(0, 1)], 1.0, 0.0)
    y_lo = jnp.where(has[(0, -1)], 1.0, 0.0)
    y_ok = jnp.where(sub < size_y, 1.0, jnp.where(sub < size_y + HALO, y_hi, y_lo))
    half = STEP_DT * y_ok

    def span(j):
        if n_gx == 2:
            gone = j - j % 2
            return jnp.where(has_lo, gone - HALO, 0), (rows_w - gone) // 2, 2
        return start, 8, rows_w // 8


    def coefficients(k, carry):
        for i in range(rows_w // 4):
            x = start + k * (rows_w // 4) + i
            ok = y_ok * jnp.where(jnp.logical_or(x < size_x, has_hi), 1.0, 0.0)
            for c in range(2):
                rate = 0.25 * cw[c, x + LOW]
                scaled = ok / (1.0 + rate)
                drive[c, x + LOW] = STEP_DT * scaled
                decay[c, x + LOW] = (1.0 - rate) * scaled
        return carry

    lax.fori_loop(0, 4, coefficients, 0)

    def y_next(f):
        return pltpu.roll(f, wy - 1, 0)

    def y_prev(f):
        return pltpu.roll(f, 1, 0)

    def z_next(f):
        return jnp.where(lane == depth - 1, 0.0, pltpu.roll(f, depth - 1, 1))

    def z_prev(f):
        return jnp.where(lane == 0, 0.0, pltpu.roll(f, 1, 1))

    def step_rows(r, chunk, e_src, h, e_dst, after):
        ex, ey, ez = (e_src[c, r] for c in range(3))
        hp_y, hp_z = h[1, r - 1], h[2, r - 1]
        for i in range(chunk):
            ey_n, ez_n = e_src[1, r + i + 1], e_src[2, r + i + 1]
            ex_n = e_src[0, r + i + 1] if i < chunk - 1 else None
            hx = h[0, r + i] - half * ((y_next(ez) - ez) - (z_next(ey) - ey))
            hy = h[1, r + i] - half * ((z_next(ex) - ex) - (ez_n - ez))
            hz = h[2, r + i] - half * ((ey_n - ey) - (y_next(ex) - ex))
            h[0, r + i] = hx
            h[1, r + i] = hy
            h[2, r + i] = hz
            cx = (hz - y_prev(hz)) - (hy - z_prev(hy))
            cy = (hx - z_prev(hx)) - (hz - hp_z)
            cz = (hy - hp_y) - (hx - y_prev(hx))
            hp_y, hp_z = hy, hz
            dec_h, drv_h = decay[0, r + i], drive[0, r + i]
            dec_v, drv_v = decay[1, r + i], drive[1, r + i]
            new = (dec_h * ex + drv_h * cx, dec_h * ey + drv_h * cy, dec_v * ez + drv_v * cz)
            for c in range(3):
                e_dst[c, r + i] = new[c]
            if after is not None:
                after(r + i, new)
            ex, ey, ez = ex_n, ey_n, ez_n

    def step(j, e_src, h, e_dst, after=None):
        first, chunk, chunks = span(j)

        def body(k, carry):
            step_rows(first + LOW + k * chunk, chunk, e_src, h, e_dst, after)
            return carry

        lax.fori_loop(0, chunks, body, 0)

    each_dir(lambda d: halo_copy(3, d).start(), to_side)
    wait_in(2)
    for n in range(STEPS):
        step(n, fw.at[0:3] if n == 0 else kept.at[n - 1], fw.at[3:6], kept.at[n])

    rec = jnp.zeros((size_y, depth), jnp.float32)
    for n in range(STEPS):
        for c in range(2):
            for x in range(size_x):
                at = (2 * n + c) * size_x + x
                e = kept[n, c, LOW + x, 0:size_y]
                rec = jnp.where(lanes == at, pltpu.roll(e, (at - ZREC) % depth, 1), rec)
    inj_own[...] = count * rec - obs_sum

    def inj_copy(d):
        dx, dy = DIRS[d]
        return pltpu.make_async_remote_copy(
            src_ref=inj_own, dst_ref=inj_in.at[(1 - dx) * 3 + 1 - dy],
            send_sem=inj_send.at[d], recv_sem=inj_recv.at[d],
            device_id={"gx": ix + dx, "gy": iy + dy}, device_id_type=MESH,
        )

    each_dir(lambda d: inj_copy(d).start(), to_side)

    at_rec = lax.dot_general(in_y, rec, over0, precision=highest, preferred_element_type=jnp.float32)
    resid = at_x * at_rec - obs_l
    mis_own[...] = 0.5 * jnp.sum((resid * resid).reshape(rpt // 8, 8, depth), axis=0)

    def mis_copy(k):
        return pltpu.make_async_remote_copy(
            src_ref=mis_own, dst_ref=mis_in.at[k],
            send_sem=mis_send.at[k], recv_sem=mis_recv.at[k],
            device_id=plane_partner(k), device_id_type=MESH,
        )

    for k in range(1, n_gx * n_gy):
        mis_copy(k).start()

    wait_in(3)
    each_dir(lambda d: inj_copy(d).wait_recv(), from_side)
    sub8 = lax.broadcasted_iota(jnp.int32, (2 * HALO, depth), 0)
    for q in range(3):
        own = inj_own[...] if q == 1 else inj_in[q * 3 + 1]
        inj_win[q, 0:size_y] = own
        inj_win[q, size_y:wy] = jnp.where(
            sub8 < HALO,
            inj_in[q * 3 + 2, 0 : 2 * HALO],
            inj_in[q * 3, size_y - 2 * HALO : size_y],
        )

    for n in reversed(range(STEPS)):
        deep = n + 1
        for x in range(-deep, size_x + deep):
            for c in range(2):
                at = (2 * n + c) * size_x + x % size_x
                moved = pltpu.roll(inj_win[x // size_x + 1], (ZREC - at) % depth, 1)
                aw[c, x + LOW] = aw[c, x + LOW] + jnp.where(lane == ZREC, moved, 0.0)

        def add_gradient(r, new, n=n):
            tile = slice(0, size_y)
            g_h = new[0][tile] * kept[n, 0, r, tile] + new[1][tile] * kept[n, 1, r, tile]
            g_v = new[2][tile] * kept[n, 2, r, tile]
            if n < STEPS - 1:
                g_h = grad[0, r] + g_h
                g_v = grad[1, r] + g_v
            grad[0, r] = g_h
            grad[1, r] = g_v

        step(STEPS - 1 - n, aw.at[0:3], aw.at[3:6], aw.at[0:3], add_gradient)

    for k in range(1, n_gx * n_gy):
        mis_copy(k).wait_recv()
    misfit = mis_own[...]
    for k in range(1, n_gx * n_gy):
        misfit = misfit + mis_in[k]

    flag = footprint[0, 0, 0].astype(jnp.float32)
    block = size_x // n_tx
    cells_rows = 2 * block * size_y

    def ordered(dst, dz, to_core):
        z = z_partner(dz)
        first = owner[0, 0, 2 * z + to_core] * block
        for c in range(2):
            for b in range(block):
                at = (c * block + b) * size_y
                dst[dz, at : at + size_y] = flag * grad[c, LOW + first + b]
        dst[dz, cells_rows : cells_rows + 8] = misfit

    def sib_copy(dz):
        return pltpu.make_async_remote_copy(
            src_ref=give.at[dz], dst_ref=got.at[dz],
            send_sem=sib_send.at[dz], recv_sem=sib_recv.at[dz],
            device_id=sibling, device_id_type=MESH,
        )

    def z_copy(dz):
        return pltpu.make_async_remote_copy(
            src_ref=keep.at[dz], dst_ref=part.at[dz],
            send_sem=z_send.at[dz], recv_sem=z_recv.at[dz],
            device_id={"tx": 2 * z_partner(dz) + core}, device_id_type=MESH,
        )

    order = list(range(1, nz)) + [0]
    for dz in order:
        ordered(give, dz, 1 - core)
        sib_copy(dz).start()
    for dz in order:
        ordered(keep, dz, core)
    for dz in order:
        sib_copy(dz).wait_recv()
        keep[dz] = keep[dz] + got[dz]
        if dz:
            z_copy(dz).start()
    for dz in range(1, nz):
        z_copy(dz).wait_recv()
    total = keep[0]
    for dz in range(1, nz):
        total = total + part[dz]
    for c in range(2):
        for b in range(block):
            at = (c * block + b) * size_y
            out[0, 0, c, b] = total[at : at + size_y]
    misfit_out[0, 0] = jnp.sum(total[cells_rows : cells_rows + 8])

    for which in range(4):
        each_dir(lambda d, w=which: halo_copy(w, d).wait_send(), to_side)
    each_dir(lambda d: inj_copy(d).wait_send(), to_side)
    for k in range(1, n_gx * n_gy):
        mis_copy(k).wait_send()
    for dz in order:
        sib_copy(dz).wait_send()
    for dz in range(1, nz):
        z_copy(dz).wait_send()


def on_device(sizes, cond_h, cond_v, fwd_init, adj_init, observed, footprint, owner, rec_cells):
    n_tx, n_gx, n_gy = sizes
    nz = n_tx // 2
    size_x, size_y, depth = cond_h.shape
    rows_w = window_rows(n_gx, size_x)
    rows = LOW + rows_w + 1
    wy = size_y + 2 * HALO
    block = size_x // n_tx
    packed = 2 * block * size_y + 8
    f32 = jnp.float32
    n_dirs = len(DIRS)
    plane = n_gx * n_gy
    dma = pltpu.SemaphoreType.DMA
    hbm, vmem, smem = pl.ANY, pltpu.VMEM, pltpu.SMEM
    owned, misfit = pl.pallas_call(
        functools.partial(kernel, sizes),
        out_shape=(
            jax.ShapeDtypeStruct((1, 1, 2, block, size_y, depth), f32),
            jax.ShapeDtypeStruct((1, 1), f32),
        ),
        in_specs=[
            pl.BlockSpec(memory_space=s) for s in [hbm] * 8
        ],
        out_specs=(pl.BlockSpec(memory_space=vmem), pl.BlockSpec(memory_space=smem)),
        scratch_shapes=[
            vmem((6, rows, wy, depth), f32),
            vmem((6, rows, wy, depth), f32),
            vmem((2, rows, wy, depth), f32),
            vmem((2, rows, wy, depth), f32),
            vmem((2, rows, wy, depth), f32),
            vmem((STEPS, 3, rows, wy, depth), f32),
            vmem((2, rows, size_y, depth), f32),
            vmem((size_y, depth), f32),
            vmem((9, size_y, depth), f32),
            vmem((3, wy, depth), f32),
            vmem((2 * STEPS, depth), f32),
            vmem(observed.shape, f32),
            smem(footprint.shape, jnp.int32),
            smem(owner.shape, jnp.int32),
            vmem(rec_cells.shape, jnp.int32),
            vmem((8, depth), f32),
            vmem((plane, 8, depth), f32),
            vmem((nz, packed, depth), f32),
            vmem((nz, packed, depth), f32),
            vmem((nz, packed, depth), f32),
            vmem((nz, packed, depth), f32),
            dma((8,)),
            dma((4, n_dirs)),
            dma((4, n_dirs)),
            dma((n_dirs,)),
            dma((n_dirs,)),
            dma((plane,)),
            dma((plane,)),
            dma((nz,)),
            dma((nz,)),
            dma((nz,)),
            dma((nz,)),
        ],
        compiler_params=pltpu.CompilerParams(
            collective_id=0, has_side_effects=True, vmem_limit_bytes=60 * 1024 * 1024
        ),
    )(cond_h, cond_v, fwd_init, adj_init, observed, footprint, owner, rec_cells)
    return owned, misfit.reshape(())


def solution(mesh):
    placed = (
        P("gx", "gy", None),
        P("gx", "gy", None),
        P("tx", None, "gx", "gy", None),
        P("tx", None, "gx", "gy", None),
        P("tx", None, "gx", "gy", None, None),
        P("tx", "gx", "gy"),
        P("gx", "gy", None),
        P("gx", "gy", None),
    )
    sizes = (mesh.shape["tx"], mesh.shape["gx"], mesh.shape["gy"])
    return jax.shard_map(
        functools.partial(on_device, sizes),
        mesh=mesh,
        in_specs=placed,
        out_specs=(P("gx", "tx", None, None, "gy", None), P()),
        check_vma=False,
    )
```
